32 devices in a mesh: ctx: 16 (over z, y, x), mp: 2 (over core).
Axes of the slice: x: 2, y: 2, z: 4, core: 2. Of those that a mesh axis runs over, the one named last changes fastest.
Arguments:
- seq_in: bfloat16 [2048, 8192], P('ctx', 'mp'), may hold values from -6 to 6
- gate_in: bfloat16 [2048, 8192], P('ctx', 'mp'), may hold values from -6 to 6
- upstream: bfloat16 [2048, 8192], P('ctx', 'mp'), may hold values from -6 to 6
- forget_flags: int32 [2048], P('ctx'), may hold values 0 or 1
- conv_weight: float32 [4, 8192], P(None, 'mp'), may hold values from -3 to 3
- conv_bias: float32 [8192], P('mp'), may hold values from -3 to 3
- proj_weight: bfloat16 [8192, 544], P(('mp', 'ctx')), may hold values from -0.0625 to 0.0625
- dt_weight: bfloat16 [512, 8192], P('ctx', 'mp'), may hold values from -0.25 to 0.25
- dt_bias: float32 [8192], P('mp'), may hold values from -10 to -3
- a_log: float32 [16, 8192], P(None, 'mp'), may hold values from 0 to 2.77
- skip_gain: float32 [8192], P('mp'), may hold values from 0.5 to 1.5
Outputs:
- grad_seq: bfloat16 [2048, 8192], P('ctx', 'mp')
- grad_gate: bfloat16 [2048, 8192], P('ctx', 'mp')
- grad_dt_weight: float32 [512, 8192], P('ctx', 'mp')
- grad_conv_weight: float32 [4, 8192], P(None, ('mp', 'ctx'))
- grad_conv_bias: float32 [8192], P(('mp', 'ctx'))
- grad_dt_bias: float32 [8192], P(('mp', 'ctx'))
- grad_a_log: float32 [16, 8192], P(None, ('mp', 'ctx'))
- grad_skip: float32 [8192], P(('mp', 'ctx'))
The draws below stay inside these ranges and needn't reach their ends.
All inputs are finite; a program needn't handle non-finite values. No bound on the sum of `forget_flags` on one device may be relied on, other than what follows from the above.
Results may differ from the reference program's by a relative error of at most 0.017.
Values may be sent and summed in bfloat16 or wider, within the bound.
No kernel may reach another device: no remote copies, remote signals or barrier semaphores. Data moves between devices by JAX's collectives and lax.ppermute only.
A program may use at most 128 MiB of HBM per device.

```python
import jax
import jax.numpy as jnp
from jax import lax

DI = 8192
STATE = 16
RANK = 512
CONV = 4
PROJ = 544
TOKENS = 2048
N_MP = 2


def place_ends(drawn, key, low, high):
    longest = drawn.shape.index(max(drawn.shape))
    spots = []
    for shift in (0, 1):
        where = [jax.random.randint(jax.random.fold_in(key, axis), (), 0, length) for axis, length in enumerate(drawn.shape)]
        where[longest] = (where[longest] + shift) % drawn.shape[longest]
        spots.append(tuple(where))
    return drawn.at[spots[0]].set(low).at[spots[1]].set(high)


def block_levels(own_key, shape, pieces, least, top_value):
    level, own = 1.0, jax.random.fold_in(own_key, 6)
    for axis_at, shards_of in pieces:
        draws = jnp.exp(jax.random.uniform(jax.random.fold_in(own, axis_at), (shards_of,), jnp.float32, least / len(pieces), top_value / len(pieces)))
        level = level * jnp.repeat(draws, shape[axis_at] // shards_of).reshape([-1 if axis == axis_at else 1 for axis in range(len(shape))])
    return level


def bell_draw(stream_key, shape, scale, bound, split=(), held_as=jnp.bfloat16):
    entries = scale * jax.random.normal(stream_key, shape, jnp.float32)
    if split:
        entries = entries * block_levels(stream_key, shape, split, -0.22, 0.18)
    return jnp.clip(entries, -bound, bound).astype(held_as)


def setup_inputs(seed: int = 0) -> dict:
    streams_of = jax.random.split(jax.random.key(seed), 12)
    return {
        "seq_in": bell_draw(streams_of[0], (TOKENS, DI), 1.0, 6.0, ((0, 16), (1, 2))),
        "gate_in": bell_draw(streams_of[1], (TOKENS, DI), 1.0, 6.0, ((0, 16), (1, 2))),
        "upstream": bell_draw(streams_of[2], (TOKENS, DI), 1.0, 6.0, ((0, 16), (1, 2))),
        "forget_flags": place_ends((jax.random.randint(streams_of[3], (TOKENS,), 0, 2) < 1).astype(jnp.int32), jax.random.fold_in(streams_of[3], 1), 0, 1),
        "conv_weight": bell_draw(streams_of[4], (CONV, DI), CONV ** -0.5, 3.0, ((1, 2),), jnp.float32),
        "conv_bias": bell_draw(streams_of[5], (DI,), 0.5, 3.0, ((0, 2),), jnp.float32),
        "proj_weight": bell_draw(streams_of[6], (DI, PROJ), DI ** -0.5, 0.0625, ((0, 32),)),
        "dt_weight": bell_draw(streams_of[7], (RANK, DI), RANK ** -0.5, 0.25, ((0, 16), (1, 2))),
        "dt_bias": jnp.clip(-10.0 + 7.0 * jax.random.uniform(streams_of[8], (DI,), jnp.float32) ** block_levels(streams_of[8], (DI,), ((0, 2),), -0.2, 0.2), -10.0, -3.0),
        "a_log": jnp.clip(2.77 * jax.random.uniform(streams_of[9], (STATE, DI), jnp.float32) ** block_levels(streams_of[9], (STATE, DI), ((1, 2),), -0.2, 0.2), 0.0, 2.77),
        "skip_gain": jnp.clip(1.0 + 0.1 * jax.random.normal(streams_of[10], (DI,), jnp.float32), 0.5, 1.5),
    }


def silu_grad(values):
    sigmoid = jax.nn.sigmoid(values)
    return sigmoid * (1.0 + values * (1.0 - sigmoid))

def split_cols(array, groups):
    shaped = array.reshape(array.shape[:-1] + (groups, array.shape[-1] // groups))
    return jnp.moveaxis(shaped, -2, 0)

def join_cols(stacked):
    moved = jnp.moveaxis(stacked, 0, -2)
    return moved.reshape(moved.shape[:-2] + (moved.shape[-2] * moved.shape[-1],))

def to_blocks(arrays):
    return tuple((a.reshape((a.shape[0] // 16, 16) + a.shape[1:]) for a in arrays))

def advance(carry, inputs):
    state, a_matrix = carry
    act_now, step_now, b_now, c_now = inputs
    state = jnp.exp(step_now[None, :] * a_matrix) * state + b_now[:, None] * (step_now * act_now)[None, :]
    return ((state, a_matrix), lax.optimization_barrier(jnp.sum(c_now[:, None] * state, axis=0)))

def run_block(carry, inputs):
    return lax.scan(advance, carry, inputs)

def scan_channels(act_full, step_size, b_matrix, c_matrix, log_rates, skip):
    a_matrix = -jnp.exp(log_rates)
    length = act_full.shape[0]
    start_state = jnp.zeros(log_rates.shape, act_full.dtype)
    carry, outputs = lax.scan(jax.checkpoint(run_block), (start_state, a_matrix), to_blocks((act_full, step_size, b_matrix, c_matrix)))
    return outputs.reshape(length, -1) + skip[None, :] * act_full

def conv_forward(seq_group, conv_group, cbias_group):
    length = seq_group.shape[0]
    padded = jnp.concatenate([jnp.zeros((CONV - 1, seq_group.shape[1]), seq_group.dtype), seq_group], axis=0)
    pre_act = jnp.zeros((length, seq_group.shape[1]), jnp.float32) + cbias_group[None, :]
    for k in range(CONV):
        pre_act = pre_act + conv_group[k][None, :] * padded[k:k + length]
    return (padded, pre_act)

def reference(seq_in, gate_in, upstream, forget_flags, conv_weight, conv_bias, proj_weight, dt_weight, dt_bias, a_log, skip_gain):
    groups = N_MP
    group_cols = DI // groups
    seq_groups = split_cols(seq_in, groups)
    gate_groups = split_cols(gate_in, groups)
    up_groups = split_cols(upstream, groups)
    conv_groups = split_cols(conv_weight, groups)
    cbias_groups = split_cols(conv_bias, groups)
    dtw_groups = split_cols(dt_weight, groups)
    dtb_groups = split_cols(dt_bias, groups)
    rate_groups = split_cols(a_log, groups)
    skip_groups = split_cols(skip_gain, groups)
    projw_groups = proj_weight.reshape(groups, group_cols, PROJ)

    def first_pass(running, inputs):
        seq_group, conv_group, cbias_group, projw_group = inputs
        padded, pre_act = conv_forward(seq_group, conv_group, cbias_group)
        act_half = jax.nn.silu(pre_act).astype(jnp.bfloat16)
        return (running + jnp.dot(act_half, projw_group, preferred_element_type=jnp.float32), None)
    projected, _ = lax.scan(first_pass, jnp.zeros((TOKENS, PROJ), jnp.float32), (seq_groups, conv_groups, cbias_groups, projw_groups))
    dt_low = projected[:, :RANK].astype(jnp.bfloat16)
    b_matrix = projected[:, RANK:RANK + STATE]
    c_matrix = projected[:, RANK + STATE:]
    flag_values = forget_flags.astype(jnp.float32)

    def second_pass(running, inputs):
        seq_group, gate_group, up_group, conv_group, cbias_group, dtw_group, dtb_group, rate_group, skip_group = inputs
        padded, pre_act = conv_forward(seq_group, conv_group, cbias_group)
        act_half = jax.nn.silu(pre_act).astype(jnp.bfloat16)
        dt_pre = jnp.dot(dt_low, dtw_group, preferred_element_type=jnp.float32) + dtb_group[None, :]
        step_size = jax.nn.softplus(dt_pre)
        mixed, pull = jax.vjp(scan_channels, act_half.astype(jnp.float32), step_size, b_matrix, c_matrix, rate_group, skip_group)
        grad_out = -flag_values[:, None] * up_group.astype(jnp.float32)
        gate_full = gate_group.astype(jnp.float32)
        grad_mixed = grad_out * jax.nn.silu(gate_full)
        grad_gate = (grad_out * mixed * silu_grad(gate_full)).astype(jnp.bfloat16)
        grad_act_scan, grad_step, grad_bmat, grad_cmat, grad_rate, grad_skip = pull(grad_mixed)
        grad_pre = grad_step * jax.nn.sigmoid(dt_pre)
        grad_pre_half = grad_pre.astype(jnp.bfloat16)
        grad_dtw = lax.dot_general(dt_low, grad_pre_half, (((0,), (0,)), ((), ())), preferred_element_type=jnp.float32)
        grad_low = lax.dot_general(grad_pre_half, dtw_group, (((1,), (1,)), ((), ())), preferred_element_type=jnp.float32)
        running = running + jnp.concatenate([grad_low, grad_bmat, grad_cmat], axis=1)
        return (running, (grad_act_scan, grad_gate, grad_dtw, lax.optimization_barrier(jnp.sum(grad_pre, axis=0)), grad_rate, grad_skip))
    grad_proj, stacked = lax.scan(second_pass, jnp.zeros((TOKENS, PROJ), jnp.float32), (seq_groups, gate_groups, up_groups, conv_groups, cbias_groups, dtw_groups, dtb_groups, rate_groups, skip_groups))
    act_grads, gate_grads, dtw_grads, dtb_grads, rate_grads, skip_grads = stacked
    grad_proj_half = grad_proj.astype(jnp.bfloat16)

    def third_pass(inputs):
        seq_group, conv_group, cbias_group, projw_group, grad_act_scan = inputs
        length = seq_group.shape[0]
        padded, pre_act = conv_forward(seq_group, conv_group, cbias_group)
        grad_act = grad_act_scan + lax.dot_general(grad_proj_half, projw_group, (((1,), (1,)), ((), ())), preferred_element_type=jnp.float32)
        grad_pre_act = grad_act * silu_grad(pre_act)
        grad_padded = jnp.concatenate([grad_pre_act, jnp.zeros((CONV - 1, seq_group.shape[1]), jnp.float32)], axis=0)
        grad_seq = jnp.zeros((length, seq_group.shape[1]), jnp.float32)
        for k in range(CONV):
            grad_seq = grad_seq + conv_group[k][None, :] * grad_padded[CONV - 1 - k:CONV - 1 - k + length]
        grad_cw = jnp.stack([lax.optimization_barrier(jnp.sum(grad_pre_act * padded[k:k + length], axis=0)) for k in range(CONV)])
        return (grad_seq.astype(jnp.bfloat16), grad_cw, lax.optimization_barrier(jnp.sum(grad_pre_act, axis=0)))
    seq_grads, cw_grads, cb_grads = lax.map(third_pass, (seq_groups, conv_groups, cbias_groups, projw_groups, act_grads))
    return (join_cols(seq_grads), join_cols(gate_grads), join_cols(dtw_grads), join_cols(cw_grads), join_cols(cb_grads), join_cols(dtb_grads), join_cols(rate_grads), join_cols(skip_grads))
```

```python
import functools
import jax
import jax.numpy as jnp
from jax import lax
from jax.experimental import pallas as pl
from jax.experimental.pallas import tpu as pltpu
from jax.sharding import PartitionSpec as P

STATE = 16
RANK = 512
CONV = 4
PLANE = 4
LANES = 128
GROUP = 8
UNROLL = 4
BLOCK = 32
LOG2E = 1.4426950408889634
LN2 = 0.6931471805599453
VMEM_LIMIT = 58 * 1024 * 1024
F32 = jnp.float32
BF16 = jnp.bfloat16


def row_sums(parts):
    parts = [
        functools.reduce(jnp.add, [p[r : r + 8] for r in range(0, p.shape[0], 8)]) for p in parts
    ]
    row = lax.broadcasted_iota(jnp.int32, (8, LANES), 0)
    low = row < 4
    halves = [
        jnp.where(low, parts[k], parts[k + 4])
        + pltpu.roll(jnp.where(low, parts[k + 4], parts[k]), 4, 0)
        for k in range(4)
    ]
    second = (row & 2) == 0
    quarters = [
        jnp.where(
            second,
            halves[k] + pltpu.roll(halves[k], 6, 0),
            halves[k + 2] + pltpu.roll(halves[k + 2], 2, 0),
        )
        for k in range(2)
    ]
    return jnp.where(
        (row & 1) == 0,
        quarters[0] + pltpu.roll(quarters[0], 7, 0),
        quarters[1] + pltpu.roll(quarters[1], 1, 0),
    )


def local_kernel(b, c, low, dtw, dtb, act, g, alog, step_out, sig_out, ends_out, a2, us, gs):
    tokens, width = act.shape
    rows = width // LANES
    block = min(tokens, BLOCK)
    a2[...] = (-LOG2E * jnp.exp(alog[...])).reshape(STATE, rows, LANES)

    for column in range(0, width, 256):
        columns = slice(column, column + 256)
        sig_out[:, columns] = jnp.dot(low[...], dtw[:, columns], preferred_element_type=F32)

    def prepare(i, total):
        at = pl.ds(pl.multiple_of(i * block, block), block)
        pre = sig_out[at, :] + dtb[...]
        tail = jnp.exp(-jnp.abs(pre))
        step = jnp.maximum(pre, 0.0) + jnp.log1p(tail)
        sig_out[at, :] = jnp.where(pre >= 0.0, 1.0, tail) / (1.0 + tail)
        step_out[at] = step.reshape(block, rows, LANES)
        us[at] = (step * act[at, :].astype(F32)).reshape(block, rows, LANES)
        gs[at] = g[at, :].astype(F32).reshape(block, rows, LANES)
        return total + jnp.sum(step, axis=0, keepdims=True)

    ends_out[2 * STATE : 2 * STATE + 1, :] = lax.fori_loop(
        0, tokens // block, prepare, jnp.zeros((1, width), F32)
    )
    zeros = jnp.zeros((8, LANES), F32)
    ones = jnp.ones((8, LANES), F32)
    for r in range(0, rows, 8):
        part = slice(r, r + 8)
        for base in range(0, STATE, GROUP):

            def move(t, carry):
                h, p, lam = carry
                s, u, g_now = step_out[t, part, :], us[t, part, :], gs[t, part, :]
                h, p, lam = list(h), list(p), list(lam)
                for k in range(GROUP):
                    n = base + k
                    d = jnp.exp2(s * a2[n, part, :])
                    h[k] = d * h[k] + b[t, n : n + 1, :] * u
                    p[k] = d * p[k]
                    lam[k] = lam[k] + (c[t, n : n + 1, :] * g_now) * p[k]
                return tuple(h), tuple(p), tuple(lam)

            h, _, lam = lax.fori_loop(
                0, tokens, move, ((zeros,) * GROUP, (ones,) * GROUP, (zeros,) * GROUP),
                unroll=UNROLL,
            )
            columns = slice(r * LANES, (r + 8) * LANES)
            for k in range(GROUP):
                n = base + k
                ends_out[n : n + 1, columns] = h[k].reshape(1, 8 * LANES)
                ends_out[STATE + n : STATE + n + 1, columns] = lam[k].reshape(1, 8 * LANES)


def full_kernel(
    b, c, step, sig, act, g, alog, carries, skip,
    mixed_out, pre_out, act_out, rate_out, vec_out, bc_out,
    a2, acts, gs, hist, mixed, s1, s2, gb, gc,
):
    tokens, rows, _ = step.shape
    width = rows * LANES
    block = min(tokens, BLOCK)
    dense, flat = (block, rows, LANES), (block, width)
    a2[...] = (-LOG2E * jnp.exp(alog[...])).reshape(STATE, rows, LANES)

    @pl.loop(0, tokens // block)
    def _(i):
        at = pl.ds(pl.multiple_of(i * block, block), block)
        acts[at] = act[at, :].astype(F32).reshape(dense)
        gs[at] = g[at, :].astype(F32).reshape(dense)

    carry_dense = carries[...].reshape(2 * STATE, rows, LANES)
    skip_dense = skip[...].reshape(rows, LANES)
    zero = jnp.zeros((rows, LANES), F32)

    for base in range(0, STATE, GROUP):
        group = slice(base, base + GROUP)

        def forward(t, h):
            s = step[t]
            u = s * acts[t]
            g_now = gs[t]
            h = list(h)
            total = skip_dense * acts[t] if base == 0 else mixed[t]
            for k in range(GROUP):
                n = base + k
                d = jnp.exp2(s * a2[n])
                h[k] = d * h[k] + b[t, n : n + 1, :] * u
                hist[t + 1, k] = h[k]
                total = total + c[t, n : n + 1, :] * h[k]
            mixed[t] = total
            gc[t, group, :] = row_sums([g_now * part for part in h])
            return tuple(h)

        hist[0] = carry_dense[group]
        lax.fori_loop(
            0, tokens, forward, tuple(carry_dense[base + k] for k in range(GROUP)), unroll=UNROLL
        )

        def backward(i, carry):
            m, ga = carry
            m, ga = list(m), list(ga)
            t = tokens - 1 - i
            s = step[t]
            u = s * acts[t]
            g_now = gs[t]
            total1 = zero if base == 0 else s1[t]
            total2 = zero if base == 0 else s2[t]
            products = []
            for k in range(GROUP):
                n = base + k
                lam = c[t, n : n + 1, :] * g_now + m[k]
                total1 = total1 + b[t, n : n + 1, :] * lam
                products.append(lam * u)
                m[k] = jnp.exp2(s * a2[n]) * lam
                q = m[k] * hist[t, k]
                total2 = total2 + q * a2[n]
                ga[k] = ga[k] + q * s
            gb[t, group, :] = row_sums(products)
            s1[t] = total1
            s2[t] = total2
            return tuple(m), tuple(ga)

        _, ga = lax.fori_loop(
            0, tokens, backward,
            (tuple(carry_dense[STATE + base + k] for k in range(GROUP)), (zero,) * GROUP),
            unroll=UNROLL,
        )
        for k in range(GROUP):
            n = base + k
            rate_out[n : n + 1, :] = (LN2 * a2[n] * ga[k]).reshape(1, width)

    lane = lax.broadcasted_iota(jnp.int32, (1, STATE, LANES), 2)
    state = lax.broadcasted_iota(jnp.int32, (1, STATE, LANES), 1)
    ones = jnp.ones((LANES, LANES), BF16)

    def finish(i, totals):
        at = pl.ds(pl.multiple_of(i * block, block), block)
        first, act_now, g_now = s1[at], acts[at], gs[at]
        mixed_out[at, :] = mixed[at].reshape(flat).astype(BF16)
        grad_pre = (LN2 * s2[at] + first * act_now).reshape(flat) * sig[at, :]
        pre_out[at, :] = grad_pre.astype(BF16)
        act_out[at, :] = (first * step[at] + skip_dense[None] * g_now).reshape(flat)
        both = jnp.zeros((block, LANES), F32)
        for offset, ref in ((0, gb), (STATE, gc)):
            sums = jnp.dot(
                ref[at].reshape(block * STATE, LANES).astype(BF16), ones,
                preferred_element_type=F32,
            ).reshape(block, STATE, LANES)
            both = both + jnp.sum(jnp.where(lane == state + offset, sums, 0.0), axis=1)
        bc_out[at, :] = both
        return (
            totals[0] + jnp.sum(grad_pre, axis=0, keepdims=True),
            totals[1] + jnp.sum(g_now * act_now, axis=0),
        )

    bias, gain = lax.fori_loop(
        0, tokens // block, finish, (jnp.zeros((1, width), F32), zero)
    )
    vec_out[0:1, :] = bias
    vec_out[1:2, :] = gain.reshape(1, width)


def scan_local(b, c, low, dtw, dtb, act, g, alog):
    tokens, channels = act.shape
    dense = (tokens, channels // LANES, LANES)
    operands = (b, c, low, dtw, dtb, act, g, alog)
    return pl.pallas_call(
        local_kernel,
        in_specs=[pl.BlockSpec(memory_space=pltpu.VMEM)] * len(operands),
        out_shape=[
            jax.ShapeDtypeStruct(dense, F32),
            jax.ShapeDtypeStruct((tokens, channels), F32),
            jax.ShapeDtypeStruct((2 * STATE + 1, channels), F32),
        ],
        scratch_shapes=[
            pltpu.VMEM((STATE,) + dense[1:], F32), pltpu.VMEM(dense, F32), pltpu.VMEM(dense, F32),
        ],
        compiler_params=pltpu.CompilerParams(vmem_limit_bytes=VMEM_LIMIT),
        name="scan_local",
    )(*operands)


def scan_full(b, c, step, sig, act, g, alog, carries, skip):
    tokens, channels = act.shape
    dense = (tokens, channels // LANES, LANES)
    flat = (tokens, channels)
    operands = (b, c, step, sig, act, g, alog, carries, skip)
    small = pltpu.VMEM((tokens, STATE, LANES), F32)
    return pl.pallas_call(
        full_kernel,
        in_specs=[pl.BlockSpec(memory_space=pltpu.VMEM)] * len(operands),
        out_shape=[
            jax.ShapeDtypeStruct(flat, BF16),
            jax.ShapeDtypeStruct(flat, BF16),
            jax.ShapeDtypeStruct(flat, F32),
            jax.ShapeDtypeStruct((STATE, channels), F32),
            jax.ShapeDtypeStruct((2, channels), F32),
            jax.ShapeDtypeStruct((tokens, LANES), F32),
        ],
        scratch_shapes=[
            pltpu.VMEM((STATE,) + dense[1:], F32),
            pltpu.VMEM(dense, F32),
            pltpu.VMEM(dense, F32),
            pltpu.VMEM((tokens + 1, GROUP) + dense[1:], F32),
            pltpu.VMEM(dense, F32),
            pltpu.VMEM(dense, F32),
            pltpu.VMEM(dense, F32),
            small,
            small,
        ],
        compiler_params=pltpu.CompilerParams(vmem_limit_bytes=VMEM_LIMIT),
        name="scan_full",
    )(*operands)


def carry_kernel(ends, alog, out):
    count = ends.shape[0]
    a2 = -LOG2E * jnp.exp(alog[...])
    h = jnp.zeros(a2.shape, F32)
    for j in range(count):
        out[j, :STATE, :] = h
        decay = jnp.exp2(a2 * ends[j, 2 * STATE : 2 * STATE + 1, :])
        h = decay * h + ends[j, :STATE, :]
    lam = jnp.zeros(a2.shape, F32)
    for j in reversed(range(count)):
        out[j, STATE:, :] = lam
        decay = jnp.exp2(a2 * ends[j, 2 * STATE : 2 * STATE + 1, :])
        lam = decay * lam + ends[j, STATE : 2 * STATE, :]


def exchange_carries(ends, a_log):
    count, mine = lax.axis_size("ctx"), lax.axis_index("ctx")
    rows, channels = ends.shape
    width = channels // count
    parts = lax.all_to_all(
        ends.reshape(rows, count, width).transpose(1, 0, 2), "ctx", 0, 0, tiled=True
    )
    own_rates = lax.dynamic_slice_in_dim(a_log, mine * width, width, axis=1)
    carried = pl.pallas_call(
        carry_kernel,
        out_shape=jax.ShapeDtypeStruct((count, 2 * STATE, width), F32),
        name="carry",
    )(parts, own_rates)
    back = lax.all_to_all(carried, "ctx", 0, 0, tiled=True)
    return back.transpose(1, 0, 2).reshape(2 * STATE, channels)


def shifted(block, axis, distance):
    devices = range(lax.axis_size(axis))
    route = [(i - distance, i) for i in devices if i - distance in devices]
    return lax.ppermute(block, axis, route)


def send(x, route, dtype=None):
    if dtype is None:
        return lax.ppermute(x, "ctx", route)
    return lax.ppermute(x.astype(dtype), "ctx", route).astype(x.dtype)


def flip_route(bit):
    return [(i, i ^ bit) for i in range(lax.axis_size("ctx"))]


def line_route(k):
    count = lax.axis_size("ctx")
    return [(i, (i + PLANE * k) % count) for i in range(count)]


def swap_mp(x):
    return lax.ppermute(x, "mp", [(0, 1), (1, 0)])


def plane_groups():
    count = lax.axis_size("ctx")
    return [list(range(i, i + PLANE)) for i in range(0, count, PLANE)]


def in_plane(x):
    return lax.all_to_all(x, "ctx", 0, 0, axis_index_groups=plane_groups(), tiled=True)


def by_owner(x):
    count = lax.axis_size("ctx")
    rows, channels = x.shape
    x = x.reshape(rows, count // PLANE, PLANE, channels // count).transpose(2, 0, 1, 3)
    return x.reshape(PLANE, rows, channels // PLANE)


def to_channels(x):
    rows, channels = x.shape
    return in_plane(by_owner(x)).reshape(PLANE * rows, channels // PLANE)


def to_tokens(x):
    count = lax.axis_size("ctx")
    rows, channels = x.shape
    x = in_plane(x.reshape(PLANE, rows // PLANE, channels))
    x = x.reshape(PLANE, rows // PLANE, count // PLANE, PLANE * channels // count)
    return x.transpose(1, 2, 0, 3).reshape(rows // PLANE, PLANE * channels)


def own_channels(x):
    count = lax.axis_size("ctx")
    rows, channels = x.shape
    x = x.reshape(rows, count // PLANE, PLANE, channels // count)
    x = lax.dynamic_index_in_dim(x, lax.axis_index("ctx") % PLANE, 2, keepdims=False)
    return x.reshape(rows, channels // PLANE)


def gather_line(x):
    planes = lax.axis_size("ctx") // PLANE
    mine = lax.axis_index("ctx") // PLANE
    rows = x.shape[0]
    out = jnp.zeros((planes * rows, x.shape[1]), x.dtype)
    for k in range(planes):
        block = send(x, line_route(-k)) if k else x
        out = lax.dynamic_update_slice(out, block, (lax.rem(mine + k, planes) * rows, 0))
    return out


def pick(x, at, axis=0):
    return lax.dynamic_index_in_dim(x, at, axis, keepdims=False)


def sum_plane(x):
    core = lax.axis_index("mp")
    halves = x.reshape(2, x.shape[0] // 2, x.shape[1])
    mine = pick(halves, core) + swap_mp(pick(halves, 1 - core))
    middle = mine.shape[0] // 2
    a, b = mine[:middle], mine[middle:]
    a, b = a + send(a, flip_route(1), BF16), b + send(b, flip_route(2), BF16)
    a, b = a + send(a, flip_route(2), BF16), b + send(b, flip_route(1), BF16)
    mine = jnp.concatenate([a, b], axis=0)
    other = swap_mp(mine)
    return jnp.where(
        core == 0, jnp.concatenate([mine, other], axis=0), jnp.concatenate([other, mine], axis=0)
    )


def line_carries(ends, a_log):
    count = lax.axis_size("ctx")
    rates = -jnp.exp(a_log)
    state, adjoint, total = ends[:STATE], ends[STATE : 2 * STATE], ends[2 * STATE :]

    def enter(x, direction):
        x = jnp.concatenate([x, total], axis=0)
        carry = jnp.zeros((STATE, x.shape[1]), F32)
        parts = []
        for k in range(1, count // PLANE):
            step = direction * PLANE * k
            route = [(i, i + step) for i in range(count) if 0 <= i + step < count]
            parts.append(send(x, route))
        for part in reversed(parts):
            carry = jnp.exp(rates * part[STATE:]) * carry + part[:STATE]
        return carry

    return jnp.concatenate([enter(state, 1), enter(adjoint, -1)], axis=0)


def scatter_line(parts):
    planes = lax.axis_size("ctx") // PLANE
    mine = lax.axis_index("ctx") // PLANE
    total = parts(mine)
    for k in sorted(range(1, planes), key=lambda k: -min(k, planes - k)):
        total = total + send(parts(lax.rem(mine + k, planes)), line_route(k), BF16)
    return total


def sum_line(x):
    planes = lax.axis_size("ctx") // PLANE
    mine = lax.axis_index("ctx") // PLANE
    x = x.reshape(x.shape[0], planes, x.shape[1] // planes)
    total = pick(x, mine, 1)
    for k in range(1, planes):
        total = total + send(pick(x, lax.rem(mine + k, planes), 1), line_route(k))
    return total


def silu_parts(x):
    s = jax.nn.sigmoid(x)
    return x * s, s * (1.0 + x * (1.0 - s))


def conv_forward(padded, weight, bias, length):
    pre_act = jnp.zeros((length, padded.shape[1]), F32) + bias
    for k in range(CONV):
        pre_act = pre_act + weight[k][None, :] * padded[k : k + length]
    return pre_act


def conv_backward(grad_padded, weight, length):
    grad = jnp.zeros((length, grad_padded.shape[1]), F32)
    for k in range(CONV):
        grad = grad + weight[k][None, :] * grad_padded[CONV - 1 - k : CONV - 1 - k + length]
    return grad.astype(BF16)


def conv_sums(grad, padded):
    length = grad.shape[0]
    return jnp.stack(
        [jnp.sum(grad * padded[k : k + length], axis=0) for k in range(CONV)]
        + [jnp.sum(grad, axis=0)]
    )


def spread(x):
    return jnp.broadcast_to(x[:, :, None], x.shape + (LANES,))


def split_proj(projected):
    low = projected[:, :RANK].astype(BF16)
    b = spread(projected[:, RANK : RANK + STATE])
    c = spread(projected[:, RANK + STATE :])
    return low, b, c


def matmul(x, y, dims):
    return lax.dot_general(x, y, ((dims[:1], dims[1:]), ((), ())), preferred_element_type=F32)


def gate_parts(gate_in, upstream, forget_flags):
    grad_out = -forget_flags.astype(F32)[:, None] * upstream.astype(F32)
    value, slope = silu_parts(gate_in.astype(F32))
    return (grad_out * value).astype(BF16), grad_out * slope


def outputs(grad_seq, grad_gate, grad_dtw, sums):
    return (
        grad_seq, grad_gate, grad_dtw,
        sums[:CONV], sums[CONV], sums[CONV + 1], sums[CONV + 3 :], sums[CONV + 2],
    )


def plane_body(
    seq_in, gate_in, upstream, forget_flags, conv_weight, conv_bias,
    proj_weight, dt_weight, dt_bias, a_log, skip_gain,
):
    rim = CONV - 1
    seq = to_channels(seq_in)
    rows_proj = gather_line(proj_weight)
    grad_mixed, gate_factor = gate_parts(gate_in, upstream, forget_flags)
    rows_dt = gather_line(in_plane(by_owner(dt_weight)).reshape(-1, seq.shape[1]))
    grad_mixed = to_channels(grad_mixed)
    weight, bias, step_bias, rates, gain = (
        own_channels(x)
        for x in (conv_weight, conv_bias[None], dt_bias[None], a_log, skip_gain[None])
    )
    length = seq.shape[0]
    padded = jnp.concatenate([shifted(seq[length - rim :], "ctx", PLANE), seq], axis=0)
    pre_act = conv_forward(padded, weight, bias, length)
    act = jax.nn.silu(pre_act).astype(BF16)
    low, b, c = split_proj(sum_plane(matmul(act, rows_proj, (1, 0))))
    step, sig, ends = scan_local(b, c, low, rows_dt, step_bias, act, grad_mixed, rates)
    carries = line_carries(ends, rates)
    mixed, grad_pre, grad_act, grad_rate, grad_vecs, grad_bc = scan_full(
        b, c, step, sig, act, grad_mixed, rates, carries, gain
    )
    grad_low = matmul(grad_pre, rows_dt, (1, 1))
    grad_proj = sum_plane(
        jnp.concatenate([grad_low, grad_bc[:, : 2 * STATE]], axis=1)
    ).astype(BF16)
    planes = lax.axis_size("ctx") // PLANE

    def dt_part(zt):
        part = lax.dynamic_slice_in_dim(low, zt * (RANK // planes), RANK // planes, axis=1)
        return matmul(part, grad_pre, (0, 0))

    grad_dtw = to_tokens(scatter_line(dt_part).astype(BF16)).astype(F32)
    grad_gate = (gate_factor * to_tokens(mixed).astype(F32)).astype(BF16)
    grad_pre_act = (grad_act + matmul(grad_proj, rows_proj, (1, 1))) * silu_parts(pre_act)[1]
    grad_padded = jnp.concatenate(
        [grad_pre_act, shifted(grad_pre_act[:rim], "ctx", -PLANE)], axis=0
    )
    grad_seq = to_tokens(conv_backward(grad_padded, weight, length))
    sums = sum_line(
        jnp.concatenate([conv_sums(grad_pre_act, padded), grad_vecs, grad_rate], axis=0)
    )
    return outputs(grad_seq, grad_gate, grad_dtw, sums)


def block_body(
    seq_in, gate_in, upstream, forget_flags, conv_weight, conv_bias,
    proj_weight, dt_weight, dt_bias, a_log, skip_gain,
):
    length = seq_in.shape[0]
    rim = CONV - 1
    padded = jnp.concatenate([shifted(seq_in[length - rim :], "ctx", 1), seq_in], axis=0)
    pre_act = conv_forward(padded, conv_weight, conv_bias[None], length)
    act = jax.nn.silu(pre_act).astype(BF16)
    rows_proj = lax.all_gather(proj_weight, "ctx", axis=0, tiled=True)
    rows_dt = lax.all_gather(dt_weight, "ctx", axis=0, tiled=True)
    low, b, c = split_proj(lax.psum(matmul(act, rows_proj, (1, 0)), "mp"))
    grad_mixed, gate_factor = gate_parts(gate_in, upstream, forget_flags)
    step, sig, ends = scan_local(b, c, low, rows_dt, dt_bias[None], act, grad_mixed, a_log)
    carries = exchange_carries(ends, a_log)
    mixed, grad_pre, grad_act, grad_rate, grad_vecs, grad_bc = scan_full(
        b, c, step, sig, act, grad_mixed, a_log, carries, skip_gain[None]
    )
    grad_gate = (gate_factor * mixed.astype(F32)).astype(BF16)
    grad_low = matmul(grad_pre, rows_dt, (1, 1))
    grad_proj = lax.psum(
        jnp.concatenate([grad_low, grad_bc[:, : 2 * STATE]], axis=1), "mp"
    ).astype(BF16)
    grad_pre_act = (grad_act + matmul(grad_proj, rows_proj, (1, 1))) * silu_parts(pre_act)[1]
    grad_padded = jnp.concatenate([grad_pre_act, shifted(grad_pre_act[:rim], "ctx", -1)], axis=0)
    grad_seq = conv_backward(grad_padded, conv_weight, length)
    scatter = lambda x, axis: lax.psum_scatter(x, "ctx", scatter_dimension=axis, tiled=True)
    grad_dtw = scatter(matmul(low, grad_pre, (0, 0)), 0)
    sums = scatter(
        jnp.concatenate([conv_sums(grad_pre_act, padded), grad_vecs, grad_rate], axis=0), 1
    )
    return outputs(grad_seq, grad_gate, grad_dtw, sums)


def solution(mesh):
    shares = mesh.shape["mp"] == 2 and mesh.shape["ctx"] in (8, 16)
    body = plane_body if shares else block_body
    return jax.shard_map(
        body,
        mesh=mesh,
        in_specs=(
            P("ctx", "mp"),
            P("ctx", "mp"),
            P("ctx", "mp"),
            P("ctx"),
            P(None, "mp"),
            P("mp"),
            P(("mp", "ctx"), None),
            P("ctx", "mp"),
            P("mp"),
            P(None, "mp"),
            P("mp"),
        ),
        out_specs=(
            P("ctx", "mp"),
            P("ctx", "mp"),
            P("ctx", "mp"),
            P(None, ("mp", "ctx")),
            P(("mp", "ctx")),
            P(("mp", "ctx")),
            P(None, ("mp", "ctx")),
            P(("mp", "ctx")),
        ),
        check_vma=False,
    )
```

```python
import functools
import jax
import jax.numpy as jnp
from jax import lax
from jax.experimental import pallas as pl
from jax.experimental.pallas import tpu as pltpu
from jax.sharding import PartitionSpec as P

STATE = 16
RANK = 512
CONV = 4
PLANE = 4
LANES = 128
GROUP = 8
UNROLL = 4
BLOCK = 32
COLUMNS = 256
LAST = 16
LOG2E = 1.4426950408889634
LN2 = 0.6931471805599453
VMEM_LIMIT = 58 * 1024 * 1024
VMEM_MIDDLE = 36 * 1024 * 1024
VMEM_SMALL = 24 * 1024 * 1024
F32 = jnp.float32
BF16 = jnp.bfloat16


def row_sums(parts):
    parts = [
        functools.reduce(jnp.add, [p[r : r + 8] for r in range(0, p.shape[0], 8)]) for p in parts
    ]
    row = lax.broadcasted_iota(jnp.int32, (8, LANES), 0)
    low = row < 4
    halves = [
        jnp.where(low, parts[k], parts[k + 4])
        + pltpu.roll(jnp.where(low, parts[k + 4], parts[k]), 4, 0)
        for k in range(4)
    ]
    second = (row & 2) == 0
    quarters = [
        jnp.where(
            second,
            halves[k] + pltpu.roll(halves[k], 6, 0),
            halves[k + 2] + pltpu.roll(halves[k + 2], 2, 0),
        )
        for k in range(2)
    ]
    return jnp.where(
        (row & 1) == 0,
        quarters[0] + pltpu.roll(quarters[0], 7, 0),
        quarters[1] + pltpu.roll(quarters[1], 1, 0),
    )


def join_halves(core, mine, other, out):
    half = mine.shape[1]
    for which, (first, second) in enumerate(((mine, other), (other, mine))):

        @pl.when(core[0] == which)
        def _():
            out[:, :half] = first[...].astype(out.dtype)
            out[:, half:] = second[...].astype(out.dtype)


def spread_rows(bc, out):
    values = bc[...].T
    high = values.astype(BF16)
    rest = values - high.astype(F32)
    middle = rest.astype(BF16)
    lowest = (rest - middle.astype(F32)).astype(BF16)
    parts = jnp.concatenate([high, middle, lowest], axis=1)
    count = bc.shape[0]
    column = lax.broadcasted_iota(jnp.int32, (3 * count, LANES), 0) % count
    for n in range(count):
        pick_n = jnp.where(column == n, 1.0, 0.0).astype(BF16)
        out[n] = jnp.dot(parts, pick_n, preferred_element_type=F32)


def local_kernel(
    core, mine, other, dtw, dtb, act, g, alog, step_out, sig_out, state_out, adjoint_out,
    a2, us, gs, spread, low, bc,
):
    tokens, width = act.shape
    rank = dtw.shape[0]
    join_halves(core, mine.at[:rank], other.at[:rank], low)
    join_halves(core, mine.at[rank:], other.at[rank:], bc)
    spread_rows(bc, spread)
    rows = width // LANES
    block = min(tokens, BLOCK)
    a2[...] = (-LOG2E * jnp.exp(alog[...])).reshape(STATE, rows, LANES)

    for column in range(0, width, 256):
        columns = slice(column, column + 256)
        sig_out[:, columns] = lax.dot_general(
            low[...], dtw[:, columns], (((0,), (0,)), ((), ())), preferred_element_type=F32
        )

    def prepare(i, total):
        at = pl.ds(pl.multiple_of(i * block, block), block)
        pre = sig_out[at, :] + dtb[...]
        tail = jnp.exp(-jnp.abs(pre))
        step = jnp.maximum(pre, 0.0) + jnp.log1p(tail)
        sig_out[at, :] = jnp.where(pre >= 0.0, 1.0, tail) / (1.0 + tail)
        step_out[at] = step.reshape(block, rows, LANES)
        us[at] = (step * act[at, :].astype(F32)).reshape(block, rows, LANES)
        gs[at] = g[at, :].astype(F32).reshape(block, rows, LANES)
        return total + jnp.sum(step, axis=0, keepdims=True)

    total = lax.fori_loop(0, tokens // block, prepare, jnp.zeros((1, width), F32))
    state_out[STATE : STATE + 1, :] = total
    adjoint_out[STATE : STATE + 1, :] = total
    zeros = jnp.zeros((8, LANES), F32)
    ones = jnp.ones((8, LANES), F32)
    for r in range(0, rows, 8):
        part = slice(r, r + 8)
        for base in range(0, STATE, GROUP):

            def move(t, carry):
                h, p, lam = carry
                s, u, g_now = step_out[t, part, :], us[t, part, :], gs[t, part, :]
                h, p, lam = list(h), list(p), list(lam)
                for k in range(GROUP):
                    n = base + k
                    d = jnp.exp2(s * a2[n, part, :])
                    h[k] = d * h[k] + spread[n, pl.ds(t, 1), :] * u
                    p[k] = d * p[k]
                    lam[k] = lam[k] + (spread[STATE + n, pl.ds(t, 1), :] * g_now) * p[k]
                return tuple(h), tuple(p), tuple(lam)

            h, _, lam = lax.fori_loop(
                0, tokens, move, ((zeros,) * GROUP, (ones,) * GROUP, (zeros,) * GROUP),
                unroll=UNROLL,
            )
            columns = slice(r * LANES, (r + 8) * LANES)
            for k in range(GROUP):
                n = base + k
                state_out[n : n + 1, columns] = h[k].reshape(1, 8 * LANES)
                adjoint_out[n : n + 1, columns] = lam[k].reshape(1, 8 * LANES)


def full_kernel(
    core, mine, other, dtw, step, sig, act, g, alog, carries, skip,
    mixed_out, pre_out, act_out, rate_out, vec_out, mine_out, other_out,
    a2, acts, gs, hist, mixed, s1, s2, gb, gc, spread, both_rows, bc,
):
    tokens, rows, _ = step.shape
    width = rows * LANES
    rank = dtw.shape[0]
    join_halves(core, mine, other, bc)
    spread_rows(bc, spread)
    block = min(tokens, BLOCK)
    dense, flat = (block, rows, LANES), (block, width)
    a2[...] = (-LOG2E * jnp.exp(alog[...])).reshape(STATE, rows, LANES)

    @pl.loop(0, tokens // block)
    def _(i):
        at = pl.ds(pl.multiple_of(i * block, block), block)
        acts[at] = act[at, :].astype(F32).reshape(dense)
        gs[at] = g[at, :].astype(F32).reshape(dense)

    carry_dense = carries[...].reshape(2 * STATE, rows, LANES)
    skip_dense = skip[...].reshape(rows, LANES)
    zero = jnp.zeros((rows, LANES), F32)

    for base in range(0, STATE, GROUP):
        group = slice(base, base + GROUP)

        def forward(t, h):
            s = step[t]
            u = s * acts[t]
            g_now = gs[t]
            h = list(h)
            total = skip_dense * acts[t] if base == 0 else mixed[t]
            for k in range(GROUP):
                n = base + k
                d = jnp.exp2(s * a2[n])
                h[k] = d * h[k] + spread[n, pl.ds(t, 1), :] * u
                hist[t + 1, k] = h[k]
                total = total + spread[STATE + n, pl.ds(t, 1), :] * h[k]
            mixed[t] = total
            gc[t, group, :] = row_sums([g_now * part for part in h])
            return tuple(h)

        hist[0] = carry_dense[group]
        lax.fori_loop(
            0, tokens, forward, tuple(carry_dense[base + k] for k in range(GROUP)), unroll=UNROLL
        )

        def backward(i, carry):
            m, ga = carry
            m, ga = list(m), list(ga)
            t = tokens - 1 - i
            s = step[t]
            u = s * acts[t]
            g_now = gs[t]
            total1 = zero if base == 0 else s1[t]
            total2 = zero if base == 0 else s2[t]
            products = []
            for k in range(GROUP):
                n = base + k
                lam = spread[STATE + n, pl.ds(t, 1), :] * g_now + m[k]
                total1 = total1 + spread[n, pl.ds(t, 1), :] * lam
                products.append(lam * u)
                m[k] = jnp.exp2(s * a2[n]) * lam
                q = m[k] * hist[t, k]
                total2 = total2 + q * a2[n]
                ga[k] = ga[k] + q * s
            gb[t, group, :] = row_sums(products)
            s1[t] = total1
            s2[t] = total2
            return tuple(m), tuple(ga)

        _, ga = lax.fori_loop(
            0, tokens, backward,
            (tuple(carry_dense[STATE + base + k] for k in range(GROUP)), (zero,) * GROUP),
            unroll=UNROLL,
        )
        for k in range(GROUP):
            n = base + k
            rate_out[n : n + 1, :] = (LN2 * a2[n] * ga[k]).reshape(1, width)

    lane = lax.broadcasted_iota(jnp.int32, (1, STATE, LANES), 2)
    state = lax.broadcasted_iota(jnp.int32, (1, STATE, LANES), 1)
    ones = jnp.ones((LANES, LANES), BF16)

    def finish(i, totals):
        at = pl.ds(pl.multiple_of(i * block, block), block)
        first, act_now, g_now = s1[at], acts[at], gs[at]
        mixed_out[at, :] = mixed[at].reshape(flat).astype(BF16)
        grad_pre = (LN2 * s2[at] + first * act_now).reshape(flat) * sig[at, :]
        pre_out[at, :] = grad_pre.astype(BF16)
        act_out[at, :] = (first * step[at] + skip_dense[None] * g_now).reshape(flat)
        both = jnp.zeros((block, LANES), F32)
        for offset, ref in ((0, gb), (STATE, gc)):
            sums = jnp.dot(
                ref[at].reshape(block * STATE, LANES).astype(BF16), ones,
                preferred_element_type=F32,
            ).reshape(block, STATE, LANES)
            both = both + jnp.sum(jnp.where(lane == state + offset, sums, 0.0), axis=1)
        both_rows[at, :] = both
        return (
            totals[0] + jnp.sum(grad_pre, axis=0, keepdims=True),
            totals[1] + jnp.sum(g_now * act_now, axis=0),
        )

    bias, gain = lax.fori_loop(
        0, tokens // block, finish, (jnp.zeros((1, width), F32), zero)
    )
    vec_out[0:1, :] = bias
    vec_out[1:2, :] = gain.reshape(1, width)
    half = tokens // 2
    for which, out in ((core[0], mine_out), (1 - core[0], other_out)):
        at = pl.ds(pl.multiple_of(which * half, half), half)
        out[:rank, :] = lax.dot_general(
            dtw[...], pre_out[at, :], (((1,), (1,)), ((), ())), preferred_element_type=F32
        )
        out[rank:, :] = both_rows[at, :].T[: 2 * STATE]


def took(microseconds):
    return pl.CostEstimate(
        flops=0, bytes_accessed=int(microseconds * 3.6e6), transcendentals=0
    )


def vmem_specs(count):
    return [pl.BlockSpec(memory_space=pltpu.VMEM)] * count


def scan_local(core, mine, other, dtw, dtb, act, g, alog):
    tokens, channels = act.shape
    dense = (tokens, channels // LANES, LANES)
    operands = (core, mine, other, dtw, dtb, act, g, alog)
    ends = jax.ShapeDtypeStruct((STATE + 1, channels), F32)
    return pl.pallas_call(
        local_kernel,
        in_specs=[pl.BlockSpec(memory_space=pltpu.SMEM)] + vmem_specs(len(operands) - 1),
        out_shape=[
            jax.ShapeDtypeStruct(dense, F32), jax.ShapeDtypeStruct((tokens, channels), F32), ends, ends,
        ],
        scratch_shapes=[
            pltpu.VMEM((STATE,) + dense[1:], F32), pltpu.VMEM(dense, F32), pltpu.VMEM(dense, F32),
            pltpu.VMEM((2 * STATE, tokens, LANES), F32), pltpu.VMEM((dtw.shape[0], tokens), BF16),
            pltpu.VMEM((2 * STATE, tokens), F32),
        ],
        compiler_params=pltpu.CompilerParams(vmem_limit_bytes=VMEM_MIDDLE),
        cost_estimate=took(22),
        name="scan_local",
    )(*operands)


def scan_full(core, mine, other, dtw, step, sig, act, g, alog, carries, skip):
    tokens, channels = act.shape
    dense = (tokens, channels // LANES, LANES)
    flat = (tokens, channels)
    operands = (
        core, mine[dtw.shape[0] :], other[dtw.shape[0] :], dtw, step, sig, act, g, alog, carries, skip
    )
    small = pltpu.VMEM((tokens, STATE, LANES), F32)
    half = jax.ShapeDtypeStruct((dtw.shape[0] + 2 * STATE, tokens // 2), F32)
    return pl.pallas_call(
        full_kernel,
        in_specs=[pl.BlockSpec(memory_space=pltpu.SMEM)] + vmem_specs(len(operands) - 1),
        out_shape=[
            jax.ShapeDtypeStruct(flat, BF16),
            jax.ShapeDtypeStruct(flat, BF16),
            jax.ShapeDtypeStruct(flat, F32),
            jax.ShapeDtypeStruct((STATE, channels), F32),
            jax.ShapeDtypeStruct((2, channels), F32),
            half,
            half,
        ],
        scratch_shapes=[
            pltpu.VMEM((STATE,) + dense[1:], F32),
            pltpu.VMEM(dense, F32),
            pltpu.VMEM(dense, F32),
            pltpu.VMEM((tokens + 1, GROUP) + dense[1:], F32),
            pltpu.VMEM(dense, F32),
            pltpu.VMEM(dense, F32),
            pltpu.VMEM(dense, F32),
            small,
            small,
            pltpu.VMEM((2 * STATE, tokens, LANES), F32),
            pltpu.VMEM((tokens, LANES), F32),
            pltpu.VMEM((2 * STATE, tokens), F32),
        ],
        compiler_params=pltpu.CompilerParams(vmem_limit_bytes=VMEM_LIMIT),
        cost_estimate=took(51),
        name="scan_full",
    )(*operands)


def carry_kernel(ends, alog, out):
    count = ends.shape[0]
    a2 = -LOG2E * jnp.exp(alog[...])
    h = jnp.zeros(a2.shape, F32)
    for j in range(count):
        out[j, :STATE, :] = h
        decay = jnp.exp2(a2 * ends[j, 2 * STATE : 2 * STATE + 1, :])
        h = decay * h + ends[j, :STATE, :]
    lam = jnp.zeros(a2.shape, F32)
    for j in reversed(range(count)):
        out[j, STATE:, :] = lam
        decay = jnp.exp2(a2 * ends[j, 2 * STATE : 2 * STATE + 1, :])
        lam = decay * lam + ends[j, STATE : 2 * STATE, :]


def exchange_carries(ends, a_log):
    count, mine = lax.axis_size("ctx"), lax.axis_index("ctx")
    rows, channels = ends.shape
    width = channels // count
    parts = lax.all_to_all(
        ends.reshape(rows, count, width).transpose(1, 0, 2), "ctx", 0, 0, tiled=True
    )
    own_rates = lax.dynamic_slice_in_dim(a_log, mine * width, width, axis=1)
    carried = pl.pallas_call(
        carry_kernel,
        out_shape=jax.ShapeDtypeStruct((count, 2 * STATE, width), F32),
        name="carry",
    )(parts, own_rates)
    back = lax.all_to_all(carried, "ctx", 0, 0, tiled=True)
    return back.transpose(1, 0, 2).reshape(2 * STATE, channels)


def shifted(block, axis, distance):
    devices = range(lax.axis_size(axis))
    route = [(i - distance, i) for i in devices if i - distance in devices]
    return lax.ppermute(block, axis, route)


def send(x, route, dtype=None):
    if dtype is None:
        return lax.ppermute(x, "ctx", route)
    return lax.ppermute(x.astype(dtype), "ctx", route).astype(x.dtype)


def flip_route(bit):
    return [(i, i ^ bit) for i in range(lax.axis_size("ctx"))]


def line_route(k):
    count = lax.axis_size("ctx")
    return [(i, (i + PLANE * k) % count) for i in range(count)]


def swap_mp(x):
    return lax.ppermute(x, "mp", [(0, 1), (1, 0)])


def plane_groups():
    count = lax.axis_size("ctx")
    return [list(range(i, i + PLANE)) for i in range(0, count, PLANE)]


def in_plane(x):
    return lax.all_to_all(x, "ctx", 0, 0, axis_index_groups=plane_groups(), tiled=True)


def pack_kernel(share, *refs):
    *inputs, out = refs
    row = 0
    for x in inputs:
        rows = slice(row, row + x.shape[0])
        row += x.shape[0]
        for q in range(PLANE):
            for z in range(out.shape[2] // share):
                source = (z * PLANE + q) * share
                out[q, rows, z * share : (z + 1) * share] = x[:, source : source + share]


def unpack_kernel(share, x, *outs):
    row = 0
    for out in outs:
        rows = slice(row, row + out.shape[0])
        row += out.shape[0]
        for q in range(PLANE):
            for z in range(x.shape[2] // share):
                target = (z * PLANE + q) * share
                out[:, target : target + share] = x[q, rows, z * share : (z + 1) * share].astype(
                    out.dtype
                )


def along_line(x):
    count = lax.axis_size("ctx")
    groups = [list(range(i, count, PLANE)) for i in range(PLANE)]
    return lax.all_to_all(x, "ctx", 0, 0, axis_index_groups=groups, tiled=True)


def by_owner(*arrays):
    channels = arrays[0].shape[1]
    rows = sum(x.shape[0] for x in arrays)
    share = channels // lax.axis_size("ctx")
    return pl.pallas_call(
        functools.partial(pack_kernel, share),
        in_specs=vmem_specs(len(arrays)),
        out_specs=vmem_specs(1)[0],
        out_shape=jax.ShapeDtypeStruct((PLANE, rows, channels // PLANE), arrays[0].dtype),
        cost_estimate=took(2),
        name="pack",
    )(*arrays)


def to_tokens(x, *results):
    channels = x.shape[2]
    share = channels * PLANE // lax.axis_size("ctx")
    return pl.pallas_call(
        functools.partial(unpack_kernel, share),
        in_specs=vmem_specs(1),
        out_specs=vmem_specs(len(results)),
        out_shape=[
            jax.ShapeDtypeStruct((rows, PLANE * channels), dtype) for rows, dtype in results
        ],
        cost_estimate=took(2),
        name="unpack",
    )(x)


def rim_before(x):
    count = lax.axis_size("ctx")
    rows, channels = x.shape
    x = x.reshape(rows, count // PLANE, PLANE, channels // count)
    parts = []
    for q in range(PLANE):
        route = [(i - 1, i + q) for i in range(PLANE, count, PLANE)]
        parts.append(send(x[:, :, q].reshape(rows, channels // PLANE), route))
    return functools.reduce(jnp.add, parts)


def own_channels(x):
    count = lax.axis_size("ctx")
    rows, channels = x.shape
    x = x.reshape(rows, count // PLANE, PLANE, channels // count)
    x = lax.dynamic_index_in_dim(x, lax.axis_index("ctx") % PLANE, 2, keepdims=False)
    return x.reshape(rows, channels // PLANE)


def line_blocks(x):
    planes = lax.axis_size("ctx") // PLANE
    return [send(x, line_route(-k)) if k else x for k in range(planes)]


def place_blocks(blocks, axis):
    planes = len(blocks)
    mine = lax.axis_index("ctx") // PLANE
    size = blocks[0].shape[axis]
    shape = list(blocks[0].shape)
    shape[axis] = planes * size
    out = jnp.zeros(shape, blocks[0].dtype)
    for k, block in enumerate(blocks):
        at = lax.rem(mine + k, planes) * size
        out = lax.dynamic_update_slice(out, block, (at, 0) if axis == 0 else (0, at))
    return out


def after(x, *earlier):
    return lax.optimization_barrier((x,) + earlier)[0]


def pick(x, at, axis=0):
    return lax.dynamic_index_in_dim(x, at, axis, keepdims=False)


def sum_plane(mine, other, *earlier):
    core = lax.axis_index("mp")
    mine = mine + swap_mp(other)
    half = after(mine.astype(BF16), *earlier)
    routes = [[(i, i ^ bits) for i in range(lax.axis_size("ctx"))] for bits in range(1, PLANE)]
    total = mine
    for route in routes:
        total = total + send(half, route).astype(F32)
    return total, swap_mp(total)


def by_halves(mine, other):
    core = lax.axis_index("mp")
    return jnp.where(
        core == 0, jnp.concatenate([mine, other], axis=1), jnp.concatenate([other, mine], axis=1)
    )


def fill_padded(moved, before, padded, columns):
    rows = padded.shape[0] // PLANE // 8 * 8
    padded[8 - before.shape[0] : 8, columns] = before[:, columns].astype(F32)
    for q in range(PLANE):
        padded[8 + q * rows : 8 + (q + 1) * rows, columns] = moved[q, :rows, columns].astype(F32)


def taps(padded, weight, bias, start, rows, columns):
    first = 8 - (CONV - 1) + start
    total = bias[:, columns]
    for k in range(CONV):
        total = total + weight[k : k + 1, columns] * padded[first + k : first + k + rows, columns]
    return total


def head_kernel(moved, before, weight, bias, act_out, padded):
    tokens, width = act_out.shape
    rows = tokens // PLANE
    for column in range(0, width, COLUMNS):
        columns = slice(column, column + COLUMNS)
        fill_padded(moved, before, padded, columns)
        for start in range(0, tokens, rows):
            value = taps(padded, weight, bias, start, rows, columns)
            act_out[start : start + rows, columns] = (value / (1.0 + jnp.exp(-value))).astype(BF16)


def conv_head(moved, before, weight, bias, rows):
    channels = moved.shape[2]
    operands = (moved, before, weight, bias)
    return pl.pallas_call(
        head_kernel,
        in_specs=vmem_specs(len(operands)),
        out_shape=jax.ShapeDtypeStruct((PLANE * rows, channels), BF16),
        out_specs=vmem_specs(1)[0],
        scratch_shapes=[pltpu.VMEM((PLANE * rows + 8, channels), F32)],
        compiler_params=pltpu.CompilerParams(vmem_limit_bytes=VMEM_SMALL),
        cost_estimate=took(4),
        name="conv_head",
    )(*operands)


def tail_kernel(
    core, mine, other, rows_proj, grad_act, moved, before, weight, bias, dt_parts,
    packed_out, sums_out, last_out, grad, padded, grad_proj,
):
    tokens, width = grad_act.shape
    rows = tokens // PLANE
    rim = CONV - 1
    join_halves(core, mine, other, grad_proj)
    dt_rows = packed_out.shape[1] - rows
    for q in range(PLANE):
        at = slice(q * dt_rows, (q + 1) * dt_rows)
        total = dt_parts[0, at, :].astype(F32)
        for z in range(1, dt_parts.shape[0]):
            total = total + dt_parts[z, at, :].astype(F32)
        packed_out[q, rows:, :] = total.astype(BF16)
    for column in range(0, width, COLUMNS):
        columns = slice(column, column + COLUMNS)
        fill_padded(moved, before, padded, columns)
        grad[:tokens, columns] = lax.dot_general(
            grad_proj[...], rows_proj[:, columns], (((0,), (0,)), ((), ())),
            preferred_element_type=F32,
        )
        grad[tokens:, columns] = jnp.zeros((8, COLUMNS), F32)
        sums = [jnp.zeros((8, COLUMNS), F32)] * (CONV + 1)
        fold = lambda x: functools.reduce(jnp.add, [x[r : r + 8] for r in range(0, x.shape[0], 8)])
        piece = rows // 4
        for start in range(0, tokens, piece):
            at = slice(start, start + piece)
            shifts = [
                padded[8 - rim + k + start : 8 - rim + k + start + piece, columns]
                for k in range(CONV)
            ]
            value = bias[:, columns]
            for k in range(CONV):
                value = value + weight[k : k + 1, columns] * shifts[k]
            s = 1.0 / (1.0 + jnp.exp(-value))
            now = (grad_act[at, columns] + grad[at, columns]) * (s * (1.0 + value * (1.0 - s)))
            grad[at, columns] = now
            for k in range(CONV):
                sums[k] = sums[k] + fold(now * shifts[k])
            sums[CONV] = sums[CONV] + fold(now)
        for k in range(CONV + 1):
            sums_out[k : k + 1, columns] = jnp.sum(sums[k], axis=0, keepdims=True)
        for start in range(0, tokens, piece):
            total = jnp.zeros((piece, COLUMNS), F32)
            for k in range(CONV):
                first = rim - k + start
                total = total + weight[k : k + 1, columns] * grad[first : first + piece, columns]
            to = start % rows
            packed_out[start // rows, to : to + piece, columns] = total.astype(BF16)
        last_out[:, columns] = total[piece - LAST :]


def conv_tail(core, mine, other, rows_proj, grad_act, moved, before, weight, bias, dt_parts):
    tokens, channels = grad_act.shape
    operands = (core, mine, other, rows_proj, grad_act, moved, before, weight, bias, dt_parts)
    return pl.pallas_call(
        tail_kernel,
        in_specs=[pl.BlockSpec(memory_space=pltpu.SMEM)] + vmem_specs(len(operands) - 1),
        out_shape=[
            jax.ShapeDtypeStruct(moved.shape, BF16),
            jax.ShapeDtypeStruct((CONV + 1, channels), F32),
            jax.ShapeDtypeStruct((LAST, channels), F32),
        ],
        scratch_shapes=[
            pltpu.VMEM((tokens + 8, channels), F32),
            pltpu.VMEM((tokens + 8, channels), F32),
            pltpu.VMEM((mine.shape[0], tokens), BF16),
        ],
        compiler_params=pltpu.CompilerParams(vmem_limit_bytes=VMEM_SMALL),
        cost_estimate=took(8),
        name="conv_tail",
    )(*operands)


def line_carries(state, adjoint, a_log):
    planes = lax.axis_size("ctx") // PLANE
    mine = lax.axis_index("ctx") // PLANE
    rates = -jnp.exp(a_log)
    parts = {}
    for k in range(1, planes):
        parts[k] = send(jnp.where(mine + k < planes, state, adjoint), line_route(k))
    entering = []
    for order, valid in (
        (range(planes - 1, 0, -1), lambda k: mine - k >= 0),
        (range(1, planes), lambda k: mine - k < 0),
    ):
        carry = jnp.zeros((STATE, state.shape[1]), F32)
        for k in order:
            new = jnp.exp(rates * parts[k][STATE:]) * carry + parts[k][:STATE]
            carry = jnp.where(valid(k), new, carry)
        entering.append(carry)
    return jnp.concatenate(entering, axis=0)


def sum_line(x):
    planes = lax.axis_size("ctx") // PLANE
    mine = lax.axis_index("ctx") // PLANE
    x = x.reshape(x.shape[0], planes, x.shape[1] // planes)
    total = pick(x, mine, 1)
    for k in range(1, planes):
        total = total + send(pick(x, lax.rem(mine + k, planes), 1), line_route(k))
    return total


def silu_parts(x):
    s = jax.nn.sigmoid(x)
    return x * s, s * (1.0 + x * (1.0 - s))


def conv_forward(padded, weight, bias, length):
    pre_act = jnp.zeros((length, padded.shape[1]), F32) + bias
    for k in range(CONV):
        pre_act = pre_act + weight[k][None, :] * padded[k : k + length]
    return pre_act


def conv_backward(grad_padded, weight, length):
    grad = jnp.zeros((length, grad_padded.shape[1]), F32)
    for k in range(CONV):
        grad = grad + weight[k][None, :] * grad_padded[CONV - 1 - k : CONV - 1 - k + length]
    return grad.astype(BF16)


def conv_sums(grad, padded):
    length = grad.shape[0]
    return jnp.stack(
        [jnp.sum(grad * padded[k : k + length], axis=0) for k in range(CONV)]
        + [jnp.sum(grad, axis=0)]
    )


def matmul(x, y, dims):
    return lax.dot_general(x, y, ((dims[:1], dims[1:]), ((), ())), preferred_element_type=F32)


def gate_parts(gate_in, upstream, forget_flags):
    grad_out = -forget_flags.astype(F32)[:, None] * upstream.astype(F32)
    value, slope = silu_parts(gate_in.astype(F32))
    return (grad_out * value).astype(BF16), grad_out * slope


def outputs(grad_seq, grad_gate, grad_dtw, sums):
    return (
        grad_seq, grad_gate, grad_dtw,
        sums[:CONV], sums[CONV], sums[CONV + 1], sums[CONV + 3 :], sums[CONV + 2],
    )


def plane_body(
    seq_in, gate_in, upstream, forget_flags, conv_weight, conv_bias,
    proj_weight, dt_weight, dt_bias, a_log, skip_gain,
):
    rim = CONV - 1
    core = lax.axis_index("mp")
    planes = lax.axis_size("ctx") // PLANE
    here = core.astype(jnp.int32).reshape(1)
    rows, dt_rows = seq_in.shape[0], dt_weight.shape[0]
    half = PLANE * rows // 2
    packed = by_owner(seq_in, dt_weight)
    proj_blocks = line_blocks(after(proj_weight.T, packed))
    moved = in_plane(packed)
    before = rim_before(seq_in[rows - rim :])
    weight, bias, step_bias, rates, gain = (
        own_channels(x)
        for x in (conv_weight, conv_bias[None], dt_bias[None], a_log, skip_gain[None])
    )
    act = conv_head(moved, before, weight, bias, rows)
    dt_plane = moved[:, rows:].reshape(PLANE * dt_rows, -1)
    grad_mixed, gate_factor = gate_parts(gate_in, upstream, forget_flags)
    mixed_packed = by_owner(grad_mixed)
    grad_mixed = in_plane(after(mixed_packed, moved)).reshape(PLANE * rows, -1)

    proj_blocks = after(tuple(proj_blocks), act, mixed_packed, dt_plane)
    rows_proj = place_blocks(proj_blocks, 1)
    dt_blocks = line_blocks(dt_plane)
    part = lambda at: matmul(rows_proj, lax.dynamic_slice_in_dim(act, at * half, half), (1, 1))
    mine, other = sum_plane(part(core), part(1 - core))
    rows_dt = place_blocks(dt_blocks, 0)
    step, sig, state, adjoint = scan_local(
        here, mine, other, rows_dt, step_bias, act, grad_mixed, rates
    )
    low = by_halves(mine[:RANK].astype(BF16), other[:RANK].astype(BF16))
    carries = line_carries(state, adjoint, rates)
    mixed, grad_pre, grad_act, grad_rate, grad_vecs, grad_mine, grad_other = scan_full(
        here, mine, other, rows_dt, step, sig, act, grad_mixed, rates, carries, gain
    )

    dtw_sums = matmul(low, grad_pre, (1, 0)).astype(BF16)
    dtw_moved = along_line(dtw_sums.reshape(planes, RANK // planes, -1))
    mine, other = sum_plane(grad_mine, grad_other, dtw_sums)
    mine, other = mine.astype(BF16), other.astype(BF16)
    first = 16
    start = jnp.where(core == 0, mine[:, :first], other[:, :first])
    first_pre = conv_forward(
        jnp.concatenate([before, moved[0, :first]], axis=0), weight, bias, first
    )
    grad_first = grad_act[:first] + matmul(start, rows_proj, (0, 0))
    following = shifted((grad_first * silu_parts(first_pre)[1])[:rim], "ctx", -PLANE)
    packed, grad_conv, last = conv_tail(
        here, mine, other, rows_proj, grad_act, moved, before, weight, bias, dtw_moved
    )
    following = after(following, last)
    late = [
        sum(weight[k] * following[j - k] for k in range(j + 1)) for j in range(rim)
    ]
    late = last + jnp.pad(jnp.stack(late), ((LAST - rim, 0), (0, 0)))
    grad_gate = in_plane(after(mixed, mine).reshape(PLANE, rows, -1))
    packed = lax.dynamic_update_slice(
        after(packed, grad_gate), late.astype(BF16)[None], (PLANE - 1, rows - LAST, 0)
    )
    returned = in_plane(packed)
    sums = sum_line(after(jnp.concatenate([grad_conv, grad_vecs, grad_rate], axis=0), packed))
    (grad_gate,) = to_tokens(after(grad_gate, packed), (rows, F32))
    grad_gate = (gate_factor * grad_gate).astype(BF16)
    grad_seq, grad_dtw = to_tokens(returned, (rows, BF16), (dt_rows, F32))
    return outputs(grad_seq, grad_gate, grad_dtw, sums)


def block_body(
    seq_in, gate_in, upstream, forget_flags, conv_weight, conv_bias,
    proj_weight, dt_weight, dt_bias, a_log, skip_gain,
):
    length = seq_in.shape[0]
    rim = CONV - 1
    padded = jnp.concatenate([shifted(seq_in[length - rim :], "ctx", 1), seq_in], axis=0)
    pre_act = conv_forward(padded, conv_weight, conv_bias[None], length)
    act = jax.nn.silu(pre_act).astype(BF16)
    rows_proj = lax.all_gather(proj_weight, "ctx", axis=0, tiled=True)
    rows_dt = lax.all_gather(dt_weight, "ctx", axis=0, tiled=True)
    projected = lax.psum(matmul(rows_proj, act, (0, 1)), "mp")
    low = projected[:RANK].astype(BF16)
    halves = (jnp.zeros((1,), jnp.int32), projected[:, : length // 2], projected[:, length // 2 :])
    grad_mixed, gate_factor = gate_parts(gate_in, upstream, forget_flags)
    step, sig, state, adjoint = scan_local(
        *halves, rows_dt, dt_bias[None], act, grad_mixed, a_log
    )
    carries = exchange_carries(jnp.concatenate([state[:STATE], adjoint], axis=0), a_log)
    mixed, grad_pre, grad_act, grad_rate, grad_vecs, first, second = scan_full(
        *halves, rows_dt, step, sig, act, grad_mixed, a_log, carries, skip_gain[None]
    )
    grad_gate = (gate_factor * mixed.astype(F32)).astype(BF16)
    grad_proj = lax.psum(jnp.concatenate([first, second], axis=1), "mp").astype(BF16)
    grad_pre_act = (grad_act + matmul(grad_proj, rows_proj, (0, 1))) * silu_parts(pre_act)[1]
    grad_padded = jnp.concatenate([grad_pre_act, shifted(grad_pre_act[:rim], "ctx", -1)], axis=0)
    grad_seq = conv_backward(grad_padded, conv_weight, length)
    scatter = lambda x, axis: lax.psum_scatter(x, "ctx", scatter_dimension=axis, tiled=True)
    grad_dtw = scatter(matmul(low, grad_pre, (1, 0)), 0)
    sums = scatter(
        jnp.concatenate([conv_sums(grad_pre_act, padded), grad_vecs, grad_rate], axis=0), 1
    )
    return outputs(grad_seq, grad_gate, grad_dtw, sums)


def solution(mesh):
    shares = mesh.shape["mp"] == 2 and mesh.shape["ctx"] in (8, 16)
    body = plane_body if shares else block_body
    return jax.shard_map(
        body,
        mesh=mesh,
        in_specs=(
            P("ctx", "mp"),
            P("ctx", "mp"),
            P("ctx", "mp"),
            P("ctx"),
            P(None, "mp"),
            P("mp"),
            P(("mp", "ctx"), None),
            P("ctx", "mp"),
            P("mp"),
            P(None, "mp"),
            P("mp"),
        ),
        out_specs=(
            P("ctx", "mp"),
            P("ctx", "mp"),
            P("ctx", "mp"),
            P(None, ("mp", "ctx")),
            P(("mp", "ctx")),
            P(("mp", "ctx")),
            P(None, ("mp", "ctx")),
            P(("mp", "ctx")),
        ),
        check_vma=False,
    )
```

```python
import functools
import jax
import jax.numpy as jnp
from jax import lax
from jax.experimental import pallas as pl
from jax.experimental.pallas import tpu as pltpu
from jax.sharding import PartitionSpec as P

STATE = 16
RANK = 512
CONV = 4
PLANE = 4
LANES = 128
GROUP = 8
UNROLL = 8
BLOCK = 32
COLUMNS = 256
LAST = 16
LOG2E = 1.4426950408889634
LN2 = 0.6931471805599453
VMEM_LIMIT = 58 * 1024 * 1024
VMEM_MIDDLE = 36 * 1024 * 1024
VMEM_SMALL = 24 * 1024 * 1024
F32 = jnp.float32
BF16 = jnp.bfloat16


def row_sums(parts):
    parts = [
        functools.reduce(jnp.add, [p[r : r + 8] for r in range(0, p.shape[0], 8)]) for p in parts
    ]
    row = lax.broadcasted_iota(jnp.int32, (8, LANES), 0)
    low = row < 4
    halves = [
        jnp.where(low, parts[k], parts[k + 4])
        + pltpu.roll(jnp.where(low, parts[k + 4], parts[k]), 4, 0)
        for k in range(4)
    ]
    second = (row & 2) == 0
    quarters = [
        jnp.where(
            second,
            halves[k] + pltpu.roll(halves[k], 6, 0),
            halves[k + 2] + pltpu.roll(halves[k + 2], 2, 0),
        )
        for k in range(2)
    ]
    return jnp.where(
        (row & 1) == 0,
        quarters[0] + pltpu.roll(quarters[0], 7, 0),
        quarters[1] + pltpu.roll(quarters[1], 1, 0),
    )


def join_halves(core, mine, other, out):
    half = mine.shape[1]
    for which, (first, second) in enumerate(((mine, other), (other, mine))):

        @pl.when(core[0] == which)
        def _():
            out[:, :half] = first[...].astype(out.dtype)
            out[:, half:] = second[...].astype(out.dtype)


def spread_rows(bc, out):
    values = bc[...].T
    high = values.astype(BF16)
    rest = values - high.astype(F32)
    middle = rest.astype(BF16)
    lowest = (rest - middle.astype(F32)).astype(BF16)
    parts = jnp.concatenate([high, middle, lowest], axis=1)
    count = bc.shape[0]
    column = lax.broadcasted_iota(jnp.int32, (3 * count, LANES), 0) % count
    for n in range(count):
        pick_n = jnp.where(column == n, 1.0, 0.0).astype(BF16)
        out[n] = jnp.dot(parts, pick_n, preferred_element_type=F32)


def local_kernel(
    core, mine, other, dtw, dtb, act, g, alog, step_out, sig_out, state_out, adjoint_out, bc,
    a2, us, gs, spread, low,
):
    tokens, width = act.shape
    rank = dtw.shape[0]
    join_halves(core, mine.at[:rank], other.at[:rank], low)
    join_halves(core, mine.at[rank:], other.at[rank:], bc)
    spread_rows(bc, spread)
    rows = width // LANES
    block = min(tokens, BLOCK)
    a2[...] = (-LOG2E * jnp.exp(alog[...])).reshape(STATE, rows, LANES)

    for column in range(0, width, 256):
        columns = slice(column, column + 256)
        sig_out[:, columns] = lax.dot_general(
            low[...], dtw[:, columns], (((0,), (0,)), ((), ())), preferred_element_type=F32
        )

    def prepare(i, total):
        at = pl.ds(pl.multiple_of(i * block, block), block)
        pre = sig_out[at, :] + dtb[...]
        tail = jnp.exp(-jnp.abs(pre))
        step = jnp.maximum(pre, 0.0) + jnp.log1p(tail)
        sig_out[at, :] = jnp.where(pre >= 0.0, 1.0, tail) / (1.0 + tail)
        step_out[at] = step.reshape(block, rows, LANES)
        us[at] = (step * act[at, :].astype(F32)).reshape(block, rows, LANES)
        gs[at] = g[at, :].astype(F32).reshape(block, rows, LANES)
        return total + jnp.sum(step, axis=0, keepdims=True)

    total = lax.fori_loop(0, tokens // block, prepare, jnp.zeros((1, width), F32))
    state_out[STATE : STATE + 1, :] = total
    adjoint_out[STATE : STATE + 1, :] = total
    zeros = jnp.zeros((8, LANES), F32)
    ones = jnp.ones((8, LANES), F32)
    for r in range(0, rows, 8):
        part = slice(r, r + 8)
        for base in range(0, STATE, GROUP):

            def move(t, carry):
                h, p, lam = carry
                s, u, g_now = step_out[t, part, :], us[t, part, :], gs[t, part, :]
                h, p, lam = list(h), list(p), list(lam)
                for k in range(GROUP):
                    n = base + k
                    d = jnp.exp2(s * a2[n, part, :])
                    h[k] = d * h[k] + spread[n, pl.ds(t, 1), :] * u
                    p[k] = d * p[k]
                    lam[k] = lam[k] + (spread[STATE + n, pl.ds(t, 1), :] * g_now) * p[k]
                return tuple(h), tuple(p), tuple(lam)

            h, _, lam = lax.fori_loop(
                0, tokens, move, ((zeros,) * GROUP, (ones,) * GROUP, (zeros,) * GROUP),
                unroll=UNROLL,
            )
            columns = slice(r * LANES, (r + 8) * LANES)
            for k in range(GROUP):
                n = base + k
                state_out[n : n + 1, columns] = h[k].reshape(1, 8 * LANES)
                adjoint_out[n : n + 1, columns] = lam[k].reshape(1, 8 * LANES)


def full_kernel(
    core, bc, dtw, step, sig, act, g, alog, carries, skip,
    mixed_out, pre_out, act_out, rate_out, vec_out, mine_out, other_out,
    a2, acts, gs, hist, mixed, s1, s2, gb, gc, spread, both_rows,
):
    tokens, rows, _ = step.shape
    width = rows * LANES
    rank = dtw.shape[0]
    spread_rows(bc, spread)
    block = min(tokens, BLOCK)
    dense, flat = (block, rows, LANES), (block, width)
    a2[...] = (-LOG2E * jnp.exp(alog[...])).reshape(STATE, rows, LANES)

    @pl.loop(0, tokens // block)
    def _(i):
        at = pl.ds(pl.multiple_of(i * block, block), block)
        acts[at] = act[at, :].astype(F32).reshape(dense)
        gs[at] = g[at, :].astype(F32).reshape(dense)

    carry_dense = carries[...].reshape(2 * STATE, rows, LANES)
    skip_dense = skip[...].reshape(rows, LANES)
    zero = jnp.zeros((rows, LANES), F32)

    for base in range(0, STATE, GROUP):
        group = slice(base, base + GROUP)

        def forward(t, h):
            s = step[t]
            u = s * acts[t]
            g_now = gs[t]
            h = list(h)
            total = skip_dense * acts[t] if base == 0 else mixed[t]
            for k in range(GROUP):
                n = base + k
                d = jnp.exp2(s * a2[n])
                h[k] = d * h[k] + spread[n, pl.ds(t, 1), :] * u
                hist[t + 1, k] = h[k]
                total = total + spread[STATE + n, pl.ds(t, 1), :] * h[k]
            mixed[t] = total
            gc[t, group, :] = row_sums([g_now * part for part in h])
            return tuple(h)

        hist[0] = carry_dense[group]
        lax.fori_loop(
            0, tokens, forward, tuple(carry_dense[base + k] for k in range(GROUP)), unroll=UNROLL
        )

        def backward(i, carry):
            m, ga = carry
            m, ga = list(m), list(ga)
            t = tokens - 1 - i
            s = step[t]
            u = s * acts[t]
            g_now = gs[t]
            total1 = zero if base == 0 else s1[t]
            total2 = zero if base == 0 else s2[t]
            products = []
            for k in range(GROUP):
                n = base + k
                lam = spread[STATE + n, pl.ds(t, 1), :] * g_now + m[k]
                total1 = total1 + spread[n, pl.ds(t, 1), :] * lam
                products.append(lam * u)
                m[k] = jnp.exp2(s * a2[n]) * lam
                q = m[k] * hist[t, k]
                total2 = total2 + q * a2[n]
                ga[k] = ga[k] + q * s
            gb[t, group, :] = row_sums(products)
            s1[t] = total1
            s2[t] = total2
            return tuple(m), tuple(ga)

        _, ga = lax.fori_loop(
            0, tokens, backward,
            (tuple(carry_dense[STATE + base + k] for k in range(GROUP)), (zero,) * GROUP),
            unroll=UNROLL,
        )
        for k in range(GROUP):
            n = base + k
            rate_out[n : n + 1, :] = (LN2 * a2[n] * ga[k]).reshape(1, width)

    lane = lax.broadcasted_iota(jnp.int32, (1, STATE, LANES), 2)
    state = lax.broadcasted_iota(jnp.int32, (1, STATE, LANES), 1)
    ones = jnp.ones((LANES, LANES), BF16)

    def finish(i, totals):
        at = pl.ds(pl.multiple_of(i * block, block), block)
        first, act_now, g_now = s1[at], acts[at], gs[at]
        mixed_out[at, :] = mixed[at].reshape(flat).astype(BF16)
        grad_pre = (LN2 * s2[at] + first * act_now).reshape(flat) * sig[at, :]
        pre_out[at, :] = grad_pre.astype(BF16)
        act_out[at, :] = (first * step[at] + skip_dense[None] * g_now).reshape(flat)
        both = jnp.zeros((block, LANES), F32)
        for offset, ref in ((0, gb), (STATE, gc)):
            sums = jnp.dot(
                ref[at].reshape(block * STATE, LANES).astype(BF16), ones,
                preferred_element_type=F32,
            ).reshape(block, STATE, LANES)
            both = both + jnp.sum(jnp.where(lane == state + offset, sums, 0.0), axis=1)
        both_rows[at, :] = both
        return (
            totals[0] + jnp.sum(grad_pre, axis=0, keepdims=True),
            totals[1] + jnp.sum(g_now * act_now, axis=0),
        )

    bias, gain = lax.fori_loop(
        0, tokens // block, finish, (jnp.zeros((1, width), F32), zero)
    )
    vec_out[0:1, :] = bias
    vec_out[1:2, :] = gain.reshape(1, width)
    half = tokens // 2
    for which, out in ((core[0], mine_out), (1 - core[0], other_out)):
        at = pl.ds(pl.multiple_of(which * half, half), half)
        out[:rank, :] = lax.dot_general(
            dtw[...], pre_out[at, :], (((1,), (1,)), ((), ())), preferred_element_type=F32
        )
        out[rank:, :] = both_rows[at, :].T[: 2 * STATE]


def took(microseconds):
    return pl.CostEstimate(
        flops=0, bytes_accessed=int(microseconds * 3.6e6), transcendentals=0
    )


def vmem_specs(count):
    return [pl.BlockSpec(memory_space=pltpu.VMEM)] * count


def scan_local(core, mine, other, dtw, dtb, act, g, alog):
    tokens, channels = act.shape
    dense = (tokens, channels // LANES, LANES)
    operands = (core, mine, other, dtw, dtb, act, g, alog)
    ends = jax.ShapeDtypeStruct((STATE + 1, channels), F32)
    return pl.pallas_call(
        local_kernel,
        in_specs=[pl.BlockSpec(memory_space=pltpu.SMEM)] + vmem_specs(len(operands) - 1),
        out_shape=[
            jax.ShapeDtypeStruct(dense, F32), jax.ShapeDtypeStruct((tokens, channels), F32), ends, ends,
            jax.ShapeDtypeStruct((2 * STATE, tokens), F32),
        ],
        scratch_shapes=[
            pltpu.VMEM((STATE,) + dense[1:], F32), pltpu.VMEM(dense, F32), pltpu.VMEM(dense, F32),
            pltpu.VMEM((2 * STATE, tokens, LANES), F32), pltpu.VMEM((dtw.shape[0], tokens), BF16),
        ],
        compiler_params=pltpu.CompilerParams(vmem_limit_bytes=VMEM_MIDDLE),
        cost_estimate=took(22),
        name="scan_local",
    )(*operands)


def scan_full(core, bc, dtw, step, sig, act, g, alog, carries, skip):
    tokens, channels = act.shape
    dense = (tokens, channels // LANES, LANES)
    flat = (tokens, channels)
    operands = (core, bc, dtw, step, sig, act, g, alog, carries, skip)
    small = pltpu.VMEM((tokens, STATE, LANES), F32)
    half = jax.ShapeDtypeStruct((dtw.shape[0] + 2 * STATE, tokens // 2), F32)
    return pl.pallas_call(
        full_kernel,
        in_specs=[pl.BlockSpec(memory_space=pltpu.SMEM)] + vmem_specs(len(operands) - 1),
        out_shape=[
            jax.ShapeDtypeStruct(flat, BF16),
            jax.ShapeDtypeStruct(flat, BF16),
            jax.ShapeDtypeStruct(flat, F32),
            jax.ShapeDtypeStruct((STATE, channels), F32),
            jax.ShapeDtypeStruct((2, channels), F32),
            half,
            half,
        ],
        scratch_shapes=[
            pltpu.VMEM((STATE,) + dense[1:], F32),
            pltpu.VMEM(dense, F32),
            pltpu.VMEM(dense, F32),
            pltpu.VMEM((tokens + 1, GROUP) + dense[1:], F32),
            pltpu.VMEM(dense, F32),
            pltpu.VMEM(dense, F32),
            pltpu.VMEM(dense, F32),
            small,
            small,
            pltpu.VMEM((2 * STATE, tokens, LANES), F32),
            pltpu.VMEM((tokens, LANES), F32),
        ],
        compiler_params=pltpu.CompilerParams(vmem_limit_bytes=VMEM_LIMIT),
        cost_estimate=took(51),
        name="scan_full",
    )(*operands)


def carry_kernel(ends, alog, out):
    count = ends.shape[0]
    a2 = -LOG2E * jnp.exp(alog[...])
    h = jnp.zeros(a2.shape, F32)
    for j in range(count):
        out[j, :STATE, :] = h
        decay = jnp.exp2(a2 * ends[j, 2 * STATE : 2 * STATE + 1, :])
        h = decay * h + ends[j, :STATE, :]
    lam = jnp.zeros(a2.shape, F32)
    for j in reversed(range(count)):
        out[j, STATE:, :] = lam
        decay = jnp.exp2(a2 * ends[j, 2 * STATE : 2 * STATE + 1, :])
        lam = decay * lam + ends[j, STATE : 2 * STATE, :]


def exchange_carries(ends, a_log):
    count, mine = lax.axis_size("ctx"), lax.axis_index("ctx")
    rows, channels = ends.shape
    width = channels // count
    parts = lax.all_to_all(
        ends.reshape(rows, count, width).transpose(1, 0, 2), "ctx", 0, 0, tiled=True
    )
    own_rates = lax.dynamic_slice_in_dim(a_log, mine * width, width, axis=1)
    carried = pl.pallas_call(
        carry_kernel,
        out_shape=jax.ShapeDtypeStruct((count, 2 * STATE, width), F32),
        name="carry",
    )(parts, own_rates)
    back = lax.all_to_all(carried, "ctx", 0, 0, tiled=True)
    return back.transpose(1, 0, 2).reshape(2 * STATE, channels)


def shifted(block, axis, distance):
    devices = range(lax.axis_size(axis))
    route = [(i - distance, i) for i in devices if i - distance in devices]
    return lax.ppermute(block, axis, route)


def send(x, route, dtype=None):
    if dtype is None:
        return lax.ppermute(x, "ctx", route)
    return lax.ppermute(x.astype(dtype), "ctx", route).astype(x.dtype)


def flip_route(bit):
    return [(i, i ^ bit) for i in range(lax.axis_size("ctx"))]


def line_route(k):
    count = lax.axis_size("ctx")
    return [(i, (i + PLANE * k) % count) for i in range(count)]


def swap_mp(x):
    return lax.ppermute(x, "mp", [(0, 1), (1, 0)])


def plane_groups():
    count = lax.axis_size("ctx")
    return [list(range(i, i + PLANE)) for i in range(0, count, PLANE)]


def in_plane(x):
    return lax.all_to_all(x, "ctx", 0, 0, axis_index_groups=plane_groups(), tiled=True)


def pack_kernel(share, *refs):
    *inputs, out = refs
    row = 0
    for x in inputs:
        rows = slice(row, row + x.shape[0])
        row += x.shape[0]
        for q in range(PLANE):
            for z in range(out.shape[2] // share):
                source = (z * PLANE + q) * share
                out[q, rows, z * share : (z + 1) * share] = x[:, source : source + share]


def unpack_kernel(share, count, x, *refs):
    late, outs = refs[:-count], refs[-count:]
    row = 0
    for at, out in enumerate(outs):
        rows = slice(row, row + out.shape[0])
        row += out.shape[0]
        for q in range(PLANE):
            for z in range(x.shape[2] // share):
                source = slice(z * share, (z + 1) * share)
                target = (z * PLANE + q) * share
                target = slice(target, target + share)
                out[:, target] = x[q, rows, source].astype(out.dtype)
                if late and at == 0:
                    last = slice(out.shape[0] - LAST, out.shape[0])
                    total = x[q, last, source].astype(F32) + late[q][:, source]
                    out[last, target] = total.astype(out.dtype)


def along_line(x):
    count = lax.axis_size("ctx")
    groups = [list(range(i, count, PLANE)) for i in range(PLANE)]
    return lax.all_to_all(x, "ctx", 0, 0, axis_index_groups=groups, tiled=True)


def by_owner(*arrays):
    channels = arrays[0].shape[1]
    rows = sum(x.shape[0] for x in arrays)
    share = channels // lax.axis_size("ctx")
    return pl.pallas_call(
        functools.partial(pack_kernel, share),
        in_specs=vmem_specs(len(arrays)),
        out_specs=vmem_specs(1)[0],
        out_shape=jax.ShapeDtypeStruct((PLANE, rows, channels // PLANE), arrays[0].dtype),
        cost_estimate=took(2),
        name="pack",
    )(*arrays)


def to_tokens(x, *results, late=()):
    channels = x.shape[2]
    share = channels * PLANE // lax.axis_size("ctx")
    return pl.pallas_call(
        functools.partial(unpack_kernel, share, len(results)),
        in_specs=vmem_specs(1 + len(late)),
        out_specs=vmem_specs(len(results)),
        out_shape=[
            jax.ShapeDtypeStruct((rows, PLANE * channels), dtype) for rows, dtype in results
        ],
        cost_estimate=took(2),
        name="unpack",
    )(x, *late)


def rim_before(x):
    count = lax.axis_size("ctx")
    rows, channels = x.shape
    x = x.reshape(rows, count // PLANE, PLANE, channels // count)
    parts = []
    for q in range(PLANE):
        route = [(i - 1, i + q) for i in range(PLANE, count, PLANE)]
        parts.append(send(x[:, :, q].reshape(rows, channels // PLANE), route))
    return functools.reduce(jnp.add, parts)


def late_rows(early):
    count = lax.axis_size("ctx")
    return [
        send(early, [(i + q, i - 1) for i in range(PLANE, count, PLANE)]) for q in range(PLANE)
    ]


def own_channels(x):
    count = lax.axis_size("ctx")
    rows, channels = x.shape
    x = x.reshape(rows, count // PLANE, PLANE, channels // count)
    x = lax.dynamic_index_in_dim(x, lax.axis_index("ctx") % PLANE, 2, keepdims=False)
    return x.reshape(rows, channels // PLANE)


def line_blocks(x):
    planes = lax.axis_size("ctx") // PLANE
    return [send(x, line_route(-k)) if k else x for k in range(planes)]


def place_blocks(blocks, axis):
    planes = len(blocks)
    mine = lax.axis_index("ctx") // PLANE
    size = blocks[0].shape[axis]
    shape = list(blocks[0].shape)
    shape[axis] = planes * size
    out = jnp.zeros(shape, blocks[0].dtype)
    for k, block in enumerate(blocks):
        at = lax.rem(mine + k, planes) * size
        out = lax.dynamic_update_slice(out, block, (at, 0) if axis == 0 else (0, at))
    return out


def after(x, *earlier):
    return lax.optimization_barrier((x,) + earlier)[0]


def pick(x, at, axis=0):
    return lax.dynamic_index_in_dim(x, at, axis, keepdims=False)


def sum_plane(mine, other, *earlier):
    core = lax.axis_index("mp")
    mine = mine + swap_mp(other)
    half = after(mine.astype(BF16), *earlier)
    routes = [[(i, i ^ bits) for i in range(lax.axis_size("ctx"))] for bits in range(1, PLANE)]
    total = mine
    for route in routes:
        total = total + send(half, route).astype(F32)
    return total, swap_mp(total)


def by_halves(mine, other):
    core = lax.axis_index("mp")
    return jnp.where(
        core == 0, jnp.concatenate([mine, other], axis=1), jnp.concatenate([other, mine], axis=1)
    )


def fill_padded(moved, before, padded, columns):
    rows = padded.shape[0] // PLANE // 8 * 8
    padded[8 - before.shape[0] : 8, columns] = before[:, columns].astype(F32)
    for q in range(PLANE):
        padded[8 + q * rows : 8 + (q + 1) * rows, columns] = moved[q, :rows, columns].astype(F32)


def taps(padded, weight, bias, start, rows, columns):
    first = 8 - (CONV - 1) + start
    total = bias[:, columns]
    for k in range(CONV):
        total = total + weight[k : k + 1, columns] * padded[first + k : first + k + rows, columns]
    return total


def head_kernel(moved, before, weight, bias, act_out, padded):
    tokens, width = act_out.shape
    rows = tokens // PLANE
    for column in range(0, width, COLUMNS):
        columns = slice(column, column + COLUMNS)
        fill_padded(moved, before, padded, columns)
        for start in range(0, tokens, rows):
            value = taps(padded, weight, bias, start, rows, columns)
            act_out[start : start + rows, columns] = (value / (1.0 + jnp.exp(-value))).astype(BF16)


def conv_head(moved, before, weight, bias, rows):
    channels = moved.shape[2]
    operands = (moved, before, weight, bias)
    return pl.pallas_call(
        head_kernel,
        in_specs=vmem_specs(len(operands)),
        out_shape=jax.ShapeDtypeStruct((PLANE * rows, channels), BF16),
        out_specs=vmem_specs(1)[0],
        scratch_shapes=[pltpu.VMEM((PLANE * rows + 8, channels), F32)],
        compiler_params=pltpu.CompilerParams(vmem_limit_bytes=VMEM_SMALL),
        cost_estimate=took(4),
        name="conv_head",
    )(*operands)


def tail_kernel(
    core, mine, other, rows_proj, grad_act, moved, before, weight, bias, dt_parts,
    packed_out, sums_out, early_out, grad, padded, grad_proj,
):
    tokens, width = grad_act.shape
    rows = tokens // PLANE
    rim = CONV - 1
    join_halves(core, mine, other, grad_proj)
    dt_rows = packed_out.shape[1] - rows
    for q in range(PLANE):
        at = slice(q * dt_rows, (q + 1) * dt_rows)
        total = dt_parts[0, at, :].astype(F32)
        for z in range(1, dt_parts.shape[0]):
            total = total + dt_parts[z, at, :].astype(F32)
        packed_out[q, rows:, :] = total.astype(BF16)
    for column in range(0, width, COLUMNS):
        columns = slice(column, column + COLUMNS)
        fill_padded(moved, before, padded, columns)
        grad[:tokens, columns] = lax.dot_general(
            grad_proj[...], rows_proj[:, columns], (((0,), (0,)), ((), ())),
            preferred_element_type=F32,
        )
        grad[tokens:, columns] = jnp.zeros((8, COLUMNS), F32)
        sums = [jnp.zeros((8, COLUMNS), F32)] * (CONV + 1)
        fold = lambda x: functools.reduce(jnp.add, [x[r : r + 8] for r in range(0, x.shape[0], 8)])
        piece = rows // 4
        for start in range(0, tokens, piece):
            at = slice(start, start + piece)
            shifts = [
                padded[8 - rim + k + start : 8 - rim + k + start + piece, columns]
                for k in range(CONV)
            ]
            value = bias[:, columns]
            for k in range(CONV):
                value = value + weight[k : k + 1, columns] * shifts[k]
            s = 1.0 / (1.0 + jnp.exp(-value))
            now = (grad_act[at, columns] + grad[at, columns]) * (s * (1.0 + value * (1.0 - s)))
            grad[at, columns] = now
            for k in range(CONV):
                sums[k] = sums[k] + fold(now * shifts[k])
            sums[CONV] = sums[CONV] + fold(now)
        for k in range(CONV + 1):
            sums_out[k : k + 1, columns] = jnp.sum(sums[k], axis=0, keepdims=True)
        for start in range(0, tokens, piece):
            total = jnp.zeros((piece, COLUMNS), F32)
            for k in range(CONV):
                first = rim - k + start
                total = total + weight[k : k + 1, columns] * grad[first : first + piece, columns]
            to = start % rows
            packed_out[start // rows, to : to + piece, columns] = total.astype(BF16)
        early_out[: LAST - rim, columns] = jnp.zeros((LAST - rim, COLUMNS), F32)
        for j in range(rim):
            early = jnp.zeros((1, COLUMNS), F32)
            for k in range(j + 1):
                early = early + weight[k : k + 1, columns] * grad[j - k : j - k + 1, columns]
            early_out[LAST - rim + j : LAST - rim + j + 1, columns] = early


def conv_tail(core, mine, other, rows_proj, grad_act, moved, before, weight, bias, dt_parts):
    tokens, channels = grad_act.shape
    operands = (core, mine, other, rows_proj, grad_act, moved, before, weight, bias, dt_parts)
    return pl.pallas_call(
        tail_kernel,
        in_specs=[pl.BlockSpec(memory_space=pltpu.SMEM)] + vmem_specs(len(operands) - 1),
        out_shape=[
            jax.ShapeDtypeStruct(moved.shape, BF16),
            jax.ShapeDtypeStruct((CONV + 1, channels), F32),
            jax.ShapeDtypeStruct((LAST, channels), F32),
        ],
        scratch_shapes=[
            pltpu.VMEM((tokens + 8, channels), F32),
            pltpu.VMEM((tokens + 8, channels), F32),
            pltpu.VMEM((mine.shape[0], tokens), BF16),
        ],
        compiler_params=pltpu.CompilerParams(vmem_limit_bytes=VMEM_SMALL),
        cost_estimate=took(8),
        name="conv_tail",
    )(*operands)


def line_carries(state, adjoint, a_log):
    planes = lax.axis_size("ctx") // PLANE
    mine = lax.axis_index("ctx") // PLANE
    rates = -jnp.exp(a_log)
    parts = {}
    for k in range(1, planes):
        parts[k] = send(jnp.where(mine + k < planes, state, adjoint), line_route(k))
    entering = []
    for order, valid in (
        (range(planes - 1, 0, -1), lambda k: mine - k >= 0),
        (range(1, planes), lambda k: mine - k < 0),
    ):
        carry = jnp.zeros((STATE, state.shape[1]), F32)
        for k in order:
            new = jnp.exp(rates * parts[k][STATE:]) * carry + parts[k][:STATE]
            carry = jnp.where(valid(k), new, carry)
        entering.append(carry)
    return jnp.concatenate(entering, axis=0)


def sum_line(x):
    planes = lax.axis_size("ctx") // PLANE
    mine = lax.axis_index("ctx") // PLANE
    x = x.reshape(x.shape[0], planes, x.shape[1] // planes)
    total = pick(x, mine, 1)
    for k in range(1, planes):
        total = total + send(pick(x, lax.rem(mine + k, planes), 1), line_route(k))
    return total


def silu_parts(x):
    s = jax.nn.sigmoid(x)
    return x * s, s * (1.0 + x * (1.0 - s))


def conv_forward(padded, weight, bias, length):
    pre_act = jnp.zeros((length, padded.shape[1]), F32) + bias
    for k in range(CONV):
        pre_act = pre_act + weight[k][None, :] * padded[k : k + length]
    return pre_act


def conv_backward(grad_padded, weight, length):
    grad = jnp.zeros((length, grad_padded.shape[1]), F32)
    for k in range(CONV):
        grad = grad + weight[k][None, :] * grad_padded[CONV - 1 - k : CONV - 1 - k + length]
    return grad.astype(BF16)


def conv_sums(grad, padded):
    length = grad.shape[0]
    return jnp.stack(
        [jnp.sum(grad * padded[k : k + length], axis=0) for k in range(CONV)]
        + [jnp.sum(grad, axis=0)]
    )


def matmul(x, y, dims):
    return lax.dot_general(x, y, ((dims[:1], dims[1:]), ((), ())), preferred_element_type=F32)


def gate_parts(gate_in, upstream, forget_flags):
    grad_out = -forget_flags.astype(F32)[:, None] * upstream.astype(F32)
    value, slope = silu_parts(gate_in.astype(F32))
    return (grad_out * value).astype(BF16), grad_out * slope


def outputs(grad_seq, grad_gate, grad_dtw, sums):
    return (
        grad_seq, grad_gate, grad_dtw,
        sums[:CONV], sums[CONV], sums[CONV + 1], sums[CONV + 3 :], sums[CONV + 2],
    )


def plane_body(
    seq_in, gate_in, upstream, forget_flags, conv_weight, conv_bias,
    proj_weight, dt_weight, dt_bias, a_log, skip_gain,
):
    rim = CONV - 1
    core = lax.axis_index("mp")
    planes = lax.axis_size("ctx") // PLANE
    here = core.astype(jnp.int32).reshape(1)
    rows, dt_rows = seq_in.shape[0], dt_weight.shape[0]
    half = PLANE * rows // 2
    packed = by_owner(seq_in, dt_weight)
    proj_blocks = line_blocks(proj_weight.T)
    moved = in_plane(packed)
    before = rim_before(seq_in[rows - rim :])
    weight, bias, step_bias, rates, gain = (
        own_channels(x)
        for x in (conv_weight, conv_bias[None], dt_bias[None], a_log, skip_gain[None])
    )
    act = conv_head(moved, before, weight, bias, rows)
    dt_plane = moved[:, rows:].reshape(PLANE * dt_rows, -1)
    grad_mixed, gate_factor = gate_parts(gate_in, upstream, forget_flags)
    mixed_packed = by_owner(grad_mixed)
    grad_mixed = in_plane(after(mixed_packed, moved)).reshape(PLANE * rows, -1)

    proj_blocks = after(tuple(proj_blocks), act, mixed_packed, dt_plane)
    rows_proj = place_blocks(proj_blocks, 1)
    dt_blocks = line_blocks(dt_plane)
    part = lambda at: matmul(rows_proj, lax.dynamic_slice_in_dim(act, at * half, half), (1, 1))
    mine, other = sum_plane(part(core), part(1 - core))
    rows_dt = place_blocks(dt_blocks, 0)
    step, sig, state, adjoint, bc = scan_local(
        here, mine, other, rows_dt, step_bias, act, grad_mixed, rates
    )
    low = by_halves(mine[:RANK].astype(BF16), other[:RANK].astype(BF16))
    carries = line_carries(state, adjoint, rates)
    mixed, grad_pre, grad_act, grad_rate, grad_vecs, grad_mine, grad_other = scan_full(
        here, bc, rows_dt, step, sig, act, grad_mixed, rates, carries, gain
    )

    dtw_sums = matmul(low, grad_pre, (1, 0)).astype(BF16)
    dtw_moved = along_line(dtw_sums.reshape(planes, RANK // planes, -1))
    mine, other = sum_plane(grad_mine, grad_other, dtw_sums)
    mine, other = mine.astype(BF16), other.astype(BF16)
    packed, grad_conv, early = conv_tail(
        here, mine, other, rows_proj, grad_act, moved, before, weight, bias, dtw_moved
    )
    grad_gate = in_plane(after(mixed, mine).reshape(PLANE, rows, -1))
    returned = in_plane(after(packed, grad_gate))
    (grad_gate,) = to_tokens(after(grad_gate, packed), (rows, F32))
    grad_gate = (gate_factor * grad_gate).astype(BF16)
    late = late_rows(after(early, grad_gate))
    sums = jnp.concatenate([grad_conv, grad_vecs, grad_rate], axis=0)
    sums = sum_line(after(sums, grad_gate))
    grad_seq, grad_dtw = to_tokens(returned, (rows, BF16), (dt_rows, F32), late=late)
    return outputs(grad_seq, grad_gate, grad_dtw, sums)


def block_body(
    seq_in, gate_in, upstream, forget_flags, conv_weight, conv_bias,
    proj_weight, dt_weight, dt_bias, a_log, skip_gain,
):
    length = seq_in.shape[0]
    rim = CONV - 1
    padded = jnp.concatenate([shifted(seq_in[length - rim :], "ctx", 1), seq_in], axis=0)
    pre_act = conv_forward(padded, conv_weight, conv_bias[None], length)
    act = jax.nn.silu(pre_act).astype(BF16)
    rows_proj = lax.all_gather(proj_weight, "ctx", axis=0, tiled=True)
    rows_dt = lax.all_gather(dt_weight, "ctx", axis=0, tiled=True)
    projected = lax.psum(matmul(rows_proj, act, (0, 1)), "mp")
    low = projected[:RANK].astype(BF16)
    halves = (jnp.zeros((1,), jnp.int32), projected[:, : length // 2], projected[:, length // 2 :])
    grad_mixed, gate_factor = gate_parts(gate_in, upstream, forget_flags)
    step, sig, state, adjoint, bc = scan_local(
        *halves, rows_dt, dt_bias[None], act, grad_mixed, a_log
    )
    carries = exchange_carries(jnp.concatenate([state[:STATE], adjoint], axis=0), a_log)
    mixed, grad_pre, grad_act, grad_rate, grad_vecs, first, second = scan_full(
        halves[0], bc, rows_dt, step, sig, act, grad_mixed, a_log, carries, skip_gain[None]
    )
    grad_gate = (gate_factor * mixed.astype(F32)).astype(BF16)
    grad_proj = lax.psum(jnp.concatenate([first, second], axis=1), "mp").astype(BF16)
    grad_pre_act = (grad_act + matmul(grad_proj, rows_proj, (0, 1))) * silu_parts(pre_act)[1]
    grad_padded = jnp.concatenate([grad_pre_act, shifted(grad_pre_act[:rim], "ctx", -1)], axis=0)
    grad_seq = conv_backward(grad_padded, conv_weight, length)
    scatter = lambda x, axis: lax.psum_scatter(x, "ctx", scatter_dimension=axis, tiled=True)
    grad_dtw = scatter(matmul(low, grad_pre, (1, 0)), 0)
    sums = scatter(
        jnp.concatenate([conv_sums(grad_pre_act, padded), grad_vecs, grad_rate], axis=0), 1
    )
    return outputs(grad_seq, grad_gate, grad_dtw, sums)


def solution(mesh):
    shares = mesh.shape["mp"] == 2 and mesh.shape["ctx"] in (8, 16)
    body = plane_body if shares else block_body
    return jax.shard_map(
        body,
        mesh=mesh,
        in_specs=(
            P("ctx", "mp"),
            P("ctx", "mp"),
            P("ctx", "mp"),
            P("ctx"),
            P(None, "mp"),
            P("mp"),
            P(("mp", "ctx"), None),
            P("ctx", "mp"),
            P("mp"),
            P(None, "mp"),
            P("mp"),
        ),
        out_specs=(
            P("ctx", "mp"),
            P("ctx", "mp"),
            P("ctx", "mp"),
            P(None, ("mp", "ctx")),
            P(("mp", "ctx")),
            P(("mp", "ctx")),
            P(None, ("mp", "ctx")),
            P(("mp", "ctx")),
        ),
        check_vma=False,
    )
```

```python
import functools
import jax
import jax.numpy as jnp
from jax import lax
from jax.experimental import pallas as pl
from jax.experimental.pallas import tpu as pltpu
from jax.sharding import PartitionSpec as P

STATE = 16
RANK = 512
CONV = 4
PLANE = 4
LANES = 128
GROUP = 8
UNROLL = 8
BLOCK = 32
COLUMNS = 256
LAST = 16
LOG2E = 1.4426950408889634
LN2 = 0.6931471805599453
VMEM_LIMIT = 58 * 1024 * 1024
VMEM_SMALL = 24 * 1024 * 1024
F32 = jnp.float32
BF16 = jnp.bfloat16


def row_sums(parts):
    parts = [
        functools.reduce(jnp.add, [p[r : r + 8] for r in range(0, p.shape[0], 8)]) for p in parts
    ]
    row = lax.broadcasted_iota(jnp.int32, (8, LANES), 0)
    low = row < 4
    halves = [
        jnp.where(low, parts[k], parts[k + 4])
        + pltpu.roll(jnp.where(low, parts[k + 4], parts[k]), 4, 0)
        for k in range(4)
    ]
    second = (row & 2) == 0
    quarters = [
        jnp.where(
            second,
            halves[k] + pltpu.roll(halves[k], 6, 0),
            halves[k + 2] + pltpu.roll(halves[k + 2], 2, 0),
        )
        for k in range(2)
    ]
    return jnp.where(
        (row & 1) == 0,
        quarters[0] + pltpu.roll(quarters[0], 7, 0),
        quarters[1] + pltpu.roll(quarters[1], 1, 0),
    )


def join_halves(core, mine, other, out):
    half = mine.shape[1]
    for which, (first, second) in enumerate(((mine, other), (other, mine))):

        @pl.when(core[0] == which)
        def _():
            out[:, :half] = first[...].astype(out.dtype)
            out[:, half:] = second[...].astype(out.dtype)


def spread_rows(bc, out):
    values = bc[...].T
    high = values.astype(BF16)
    rest = values - high.astype(F32)
    middle = rest.astype(BF16)
    lowest = (rest - middle.astype(F32)).astype(BF16)
    parts = jnp.concatenate([high, middle, lowest], axis=1)
    count = bc.shape[0]
    column = lax.broadcasted_iota(jnp.int32, (3 * count, LANES), 0) % count
    for n in range(count):
        pick_n = jnp.where(column == n, 1.0, 0.0).astype(BF16)
        out[n] = jnp.dot(parts, pick_n, preferred_element_type=F32)


def local_kernel(
    core, mine, other, dtw, dtb, act, g, alog, step_to, sig_to, state_out, adjoint_out, bc,
    a2, us, gs, spread, low, step_out, sig_out, done,
):
    tokens, width = act.shape
    rank = dtw.shape[0]
    join_halves(core, mine.at[:rank], other.at[:rank], low)
    join_halves(core, mine.at[rank:], other.at[rank:], bc)
    spread_rows(bc, spread)
    rows = width // LANES
    block = min(tokens, BLOCK)
    a2[...] = (-LOG2E * jnp.exp(alog[...])).reshape(STATE, rows, LANES)

    for column in range(0, width, 256):
        columns = slice(column, column + 256)
        sig_out[:, columns] = lax.dot_general(
            low[...], dtw[:, columns], (((0,), (0,)), ((), ())), preferred_element_type=F32
        )

    def prepare(i, total):
        at = pl.ds(pl.multiple_of(i * block, block), block)
        pre = sig_out[at, :] + dtb[...]
        tail = jnp.exp(-jnp.abs(pre))
        step = jnp.maximum(pre, 0.0) + jnp.log1p(tail)
        sig_out[at, :] = jnp.where(pre >= 0.0, 1.0, tail) / (1.0 + tail)
        step_out[at] = step.reshape(block, rows, LANES)
        us[at] = (step * act[at, :].astype(F32)).reshape(block, rows, LANES)
        gs[at] = g[at, :].astype(F32).reshape(block, rows, LANES)
        return total + jnp.sum(step, axis=0, keepdims=True)

    total = lax.fori_loop(0, tokens // block, prepare, jnp.zeros((1, width), F32))
    copies = [
        pltpu.make_async_copy(step_out, step_to, done.at[0]),
        pltpu.make_async_copy(sig_out, sig_to, done.at[1]),
    ]
    for copy in copies:
        copy.start()
    state_out[STATE : STATE + 1, :] = total
    adjoint_out[STATE : STATE + 1, :] = total
    zeros = jnp.zeros((8, LANES), F32)
    ones = jnp.ones((8, LANES), F32)
    for r in range(0, rows, 8):
        part = slice(r, r + 8)
        for base in range(0, STATE, GROUP):

            def move(t, carry):
                h, p, lam = carry
                s, u, g_now = step_out[t, part, :], us[t, part, :], gs[t, part, :]
                h, p, lam = list(h), list(p), list(lam)
                for k in range(GROUP):
                    n = base + k
                    d = jnp.exp2(s * a2[n, part, :])
                    h[k] = d * h[k] + spread[n, pl.ds(t, 1), :] * u
                    p[k] = d * p[k]
                    lam[k] = lam[k] + (spread[STATE + n, pl.ds(t, 1), :] * g_now) * p[k]
                return tuple(h), tuple(p), tuple(lam)

            h, _, lam = lax.fori_loop(
                0, tokens, move, ((zeros,) * GROUP, (ones,) * GROUP, (zeros,) * GROUP),
                unroll=UNROLL,
            )
            columns = slice(r * LANES, (r + 8) * LANES)
            for k in range(GROUP):
                n = base + k
                state_out[n : n + 1, columns] = h[k].reshape(1, 8 * LANES)
                adjoint_out[n : n + 1, columns] = lam[k].reshape(1, 8 * LANES)
    for copy in copies:
        copy.wait()


def full_kernel(
    core, bc, dtw, step, sig, act, g, alog, carries, skip,
    mixed_out, pre_out, act_out, rate_out, vec_out, mine_out, other_out,
    a2, acts, gs, hist, mixed, s1, s2, gb, gc, spread, both_rows,
):
    tokens, rows, _ = step.shape
    width = rows * LANES
    rank = dtw.shape[0]
    spread_rows(bc, spread)
    block = min(tokens, BLOCK)
    dense, flat = (block, rows, LANES), (block, width)
    a2[...] = (-LOG2E * jnp.exp(alog[...])).reshape(STATE, rows, LANES)

    @pl.loop(0, tokens // block)
    def _(i):
        at = pl.ds(pl.multiple_of(i * block, block), block)
        acts[at] = act[at, :].astype(F32).reshape(dense)
        gs[at] = g[at, :].astype(F32).reshape(dense)

    carry_dense = carries[...].reshape(2 * STATE, rows, LANES)
    skip_dense = skip[...].reshape(rows, LANES)
    zero = jnp.zeros((rows, LANES), F32)

    for base in range(0, STATE, GROUP):
        group = slice(base, base + GROUP)

        def forward(t, h):
            s = step[t]
            u = s * acts[t]
            g_now = gs[t]
            h = list(h)
            total = skip_dense * acts[t] if base == 0 else mixed[t]
            for k in range(GROUP):
                n = base + k
                d = jnp.exp2(s * a2[n])
                h[k] = d * h[k] + spread[n, pl.ds(t, 1), :] * u
                hist[t + 1, k] = h[k]
                total = total + spread[STATE + n, pl.ds(t, 1), :] * h[k]
            mixed[t] = total
            gc[t, group, :] = row_sums([g_now * part for part in h])
            return tuple(h)

        hist[0] = carry_dense[group]
        lax.fori_loop(
            0, tokens, forward, tuple(carry_dense[base + k] for k in range(GROUP)), unroll=UNROLL
        )

        def backward(i, carry):
            m, ga = carry
            m, ga = list(m), list(ga)
            t = tokens - 1 - i
            s = step[t]
            u = s * acts[t]
            g_now = gs[t]
            total1 = zero if base == 0 else s1[t]
            total2 = zero if base == 0 else s2[t]
            products = []
            for k in range(GROUP):
                n = base + k
                lam = spread[STATE + n, pl.ds(t, 1), :] * g_now + m[k]
                total1 = total1 + spread[n, pl.ds(t, 1), :] * lam
                products.append(lam * u)
                m[k] = jnp.exp2(s * a2[n]) * lam
                q = m[k] * hist[t, k]
                total2 = total2 + q * a2[n]
                ga[k] = ga[k] + q * s
            gb[t, group, :] = row_sums(products)
            s1[t] = total1
            s2[t] = total2
            return tuple(m), tuple(ga)

        _, ga = lax.fori_loop(
            0, tokens, backward,
            (tuple(carry_dense[STATE + base + k] for k in range(GROUP)), (zero,) * GROUP),
            unroll=UNROLL,
        )
        for k in range(GROUP):
            n = base + k
            rate_out[n : n + 1, :] = (LN2 * a2[n] * ga[k]).reshape(1, width)

    lane = lax.broadcasted_iota(jnp.int32, (1, STATE, LANES), 2)
    state = lax.broadcasted_iota(jnp.int32, (1, STATE, LANES), 1)
    ones = jnp.ones((LANES, LANES), BF16)

    def finish(i, totals):
        at = pl.ds(pl.multiple_of(i * block, block), block)
        first, act_now, g_now = s1[at], acts[at], gs[at]
        mixed_out[at, :] = mixed[at].reshape(flat).astype(BF16)
        grad_pre = (LN2 * s2[at] + first * act_now).reshape(flat) * sig[at, :]
        pre_out[at, :] = grad_pre.astype(BF16)
        act_out[at, :] = (first * step[at] + skip_dense[None] * g_now).reshape(flat)
        both = jnp.zeros((block, LANES), F32)
        for offset, ref in ((0, gb), (STATE, gc)):
            sums = jnp.dot(
                ref[at].reshape(block * STATE, LANES).astype(BF16), ones,
                preferred_element_type=F32,
            ).reshape(block, STATE, LANES)
            both = both + jnp.sum(jnp.where(lane == state + offset, sums, 0.0), axis=1)
        both_rows[at, :] = both
        return (
            totals[0] + jnp.sum(grad_pre, axis=0, keepdims=True),
            totals[1] + jnp.sum(g_now * act_now, axis=0),
        )

    bias, gain = lax.fori_loop(
        0, tokens // block, finish, (jnp.zeros((1, width), F32), zero)
    )
    vec_out[0:1, :] = bias
    vec_out[1:2, :] = gain.reshape(1, width)
    half = tokens // 2
    for which, out in ((core[0], mine_out), (1 - core[0], other_out)):
        at = pl.ds(pl.multiple_of(which * half, half), half)
        out[:rank, :] = lax.dot_general(
            dtw[...], pre_out[at, :], (((1,), (1,)), ((), ())), preferred_element_type=F32
        )
        out[rank:, :] = both_rows[at, :].T[: 2 * STATE]


def took(microseconds):
    return pl.CostEstimate(
        flops=0, bytes_accessed=int(microseconds * 3.6e6), transcendentals=0
    )


def vmem_specs(count):
    return [pl.BlockSpec(memory_space=pltpu.VMEM)] * count


def scan_local(core, mine, other, dtw, dtb, act, g, alog):
    tokens, channels = act.shape
    dense = (tokens, channels // LANES, LANES)
    operands = (core, mine, other, dtw, dtb, act, g, alog)
    ends = jax.ShapeDtypeStruct((STATE + 1, channels), F32)
    return pl.pallas_call(
        local_kernel,
        in_specs=[pl.BlockSpec(memory_space=pltpu.SMEM)] + vmem_specs(len(operands) - 1),
        out_shape=[
            jax.ShapeDtypeStruct(dense, F32), jax.ShapeDtypeStruct((tokens, channels), F32), ends, ends,
            jax.ShapeDtypeStruct((2 * STATE, tokens), F32),
        ],
        out_specs=[pl.BlockSpec(memory_space=pl.ANY)] * 2 + vmem_specs(3),
        scratch_shapes=[
            pltpu.VMEM((STATE,) + dense[1:], F32), pltpu.VMEM(dense, F32), pltpu.VMEM(dense, F32),
            pltpu.VMEM((2 * STATE, tokens, LANES), F32), pltpu.VMEM((dtw.shape[0], tokens), BF16),
            pltpu.VMEM(dense, F32), pltpu.VMEM((tokens, channels), F32),
            pltpu.SemaphoreType.DMA((2,)),
        ],
        compiler_params=pltpu.CompilerParams(vmem_limit_bytes=VMEM_LIMIT),
        cost_estimate=took(22),
        name="scan_local",
    )(*operands)


def scan_full(core, bc, dtw, step, sig, act, g, alog, carries, skip):
    tokens, channels = act.shape
    dense = (tokens, channels // LANES, LANES)
    flat = (tokens, channels)
    operands = (core, bc, dtw, step, sig, act, g, alog, carries, skip)
    small = pltpu.VMEM((tokens, STATE, LANES), F32)
    half = jax.ShapeDtypeStruct((dtw.shape[0] + 2 * STATE, tokens // 2), F32)
    return pl.pallas_call(
        full_kernel,
        in_specs=[pl.BlockSpec(memory_space=pltpu.SMEM)] + vmem_specs(len(operands) - 1),
        out_shape=[
            jax.ShapeDtypeStruct(flat, BF16),
            jax.ShapeDtypeStruct(flat, BF16),
            jax.ShapeDtypeStruct(flat, F32),
            jax.ShapeDtypeStruct((STATE, channels), F32),
            jax.ShapeDtypeStruct((2, channels), F32),
            half,
            half,
        ],
        scratch_shapes=[
            pltpu.VMEM((STATE,) + dense[1:], F32),
            pltpu.VMEM(dense, F32),
            pltpu.VMEM(dense, F32),
            pltpu.VMEM((tokens + 1, GROUP) + dense[1:], F32),
            pltpu.VMEM(dense, F32),
            pltpu.VMEM(dense, F32),
            pltpu.VMEM(dense, F32),
            small,
            small,
            pltpu.VMEM((2 * STATE, tokens, LANES), F32),
            pltpu.VMEM((tokens, LANES), F32),
        ],
        compiler_params=pltpu.CompilerParams(vmem_limit_bytes=VMEM_LIMIT),
        cost_estimate=took(51),
        name="scan_full",
    )(*operands)


def carry_kernel(ends, alog, out):
    count = ends.shape[0]
    a2 = -LOG2E * jnp.exp(alog[...])
    h = jnp.zeros(a2.shape, F32)
    for j in range(count):
        out[j, :STATE, :] = h
        decay = jnp.exp2(a2 * ends[j, 2 * STATE : 2 * STATE + 1, :])
        h = decay * h + ends[j, :STATE, :]
    lam = jnp.zeros(a2.shape, F32)
    for j in reversed(range(count)):
        out[j, STATE:, :] = lam
        decay = jnp.exp2(a2 * ends[j, 2 * STATE : 2 * STATE + 1, :])
        lam = decay * lam + ends[j, STATE : 2 * STATE, :]


def exchange_carries(ends, a_log):
    count, mine = lax.axis_size("ctx"), lax.axis_index("ctx")
    rows, channels = ends.shape
    width = channels // count
    parts = lax.all_to_all(
        ends.reshape(rows, count, width).transpose(1, 0, 2), "ctx", 0, 0, tiled=True
    )
    own_rates = lax.dynamic_slice_in_dim(a_log, mine * width, width, axis=1)
    carried = pl.pallas_call(
        carry_kernel,
        out_shape=jax.ShapeDtypeStruct((count, 2 * STATE, width), F32),
        name="carry",
    )(parts, own_rates)
    back = lax.all_to_all(carried, "ctx", 0, 0, tiled=True)
    return back.transpose(1, 0, 2).reshape(2 * STATE, channels)


def shifted(block, axis, distance):
    devices = range(lax.axis_size(axis))
    route = [(i - distance, i) for i in devices if i - distance in devices]
    return lax.ppermute(block, axis, route)


def send(x, route, dtype=None):
    if dtype is None:
        return lax.ppermute(x, "ctx", route)
    return lax.ppermute(x.astype(dtype), "ctx", route).astype(x.dtype)


def flip_route(bit):
    return [(i, i ^ bit) for i in range(lax.axis_size("ctx"))]


def line_route(k):
    count = lax.axis_size("ctx")
    return [(i, (i + PLANE * k) % count) for i in range(count)]


def swap_mp(x):
    return lax.ppermute(x, "mp", [(0, 1), (1, 0)])


def plane_groups():
    count = lax.axis_size("ctx")
    return [list(range(i, i + PLANE)) for i in range(0, count, PLANE)]


def in_plane(x):
    return lax.all_to_all(x, "ctx", 0, 0, axis_index_groups=plane_groups(), tiled=True)


def pack_kernel(share, *refs):
    *inputs, out = refs
    row = 0
    for x in inputs:
        rows = slice(row, row + x.shape[0])
        row += x.shape[0]
        for q in range(PLANE):
            for z in range(out.shape[2] // share):
                source = (z * PLANE + q) * share
                out[q, rows, z * share : (z + 1) * share] = x[:, source : source + share]


def unpack_kernel(share, count, x, *refs):
    late, outs = refs[:-count], refs[-count:]
    row = 0
    for at, out in enumerate(outs):
        rows = slice(row, row + out.shape[0])
        row += out.shape[0]
        for q in range(PLANE):
            for z in range(x.shape[2] // share):
                source = slice(z * share, (z + 1) * share)
                target = (z * PLANE + q) * share
                target = slice(target, target + share)
                out[:, target] = x[q, rows, source].astype(out.dtype)
                if late and at == 0:
                    last = slice(out.shape[0] - LAST, out.shape[0])
                    total = x[q, last, source].astype(F32) + late[q][:, source]
                    out[last, target] = total.astype(out.dtype)


def gate_kernel(share, x, gate, up, flags, out):
    for q in range(PLANE):
        for z in range(x.shape[2] // share):
            target = (z * PLANE + q) * share
            target = slice(target, target + share)
            value = gate[:, target].astype(F32)
            s = 1.0 / (1.0 + jnp.exp(-value))
            factor = -flags[...] * up[:, target].astype(F32) * (s * (1.0 + value * (1.0 - s)))
            mixed = x[q, :, z * share : (z + 1) * share].astype(F32)
            out[:, target] = (factor * mixed).astype(BF16)


def gate_gradient(x, gate, up, flags):
    share = x.shape[2] * PLANE // lax.axis_size("ctx")
    return pl.pallas_call(
        functools.partial(gate_kernel, share),
        in_specs=vmem_specs(4),
        out_specs=vmem_specs(1)[0],
        out_shape=jax.ShapeDtypeStruct(gate.shape, BF16),
        cost_estimate=took(4),
        name="gate_gradient",
    )(x, gate, up, flags.astype(F32)[:, None])


def along_line(x):
    count = lax.axis_size("ctx")
    groups = [list(range(i, count, PLANE)) for i in range(PLANE)]
    return lax.all_to_all(x, "ctx", 0, 0, axis_index_groups=groups, tiled=True)


def by_owner(*arrays):
    channels = arrays[0].shape[1]
    rows = sum(x.shape[0] for x in arrays)
    share = channels // lax.axis_size("ctx")
    return pl.pallas_call(
        functools.partial(pack_kernel, share),
        in_specs=vmem_specs(len(arrays)),
        out_specs=vmem_specs(1)[0],
        out_shape=jax.ShapeDtypeStruct((PLANE, rows, channels // PLANE), arrays[0].dtype),
        cost_estimate=took(2),
        name="pack",
    )(*arrays)


def to_tokens(x, *results, late=()):
    channels = x.shape[2]
    share = channels * PLANE // lax.axis_size("ctx")
    return pl.pallas_call(
        functools.partial(unpack_kernel, share, len(results)),
        in_specs=vmem_specs(1 + len(late)),
        out_specs=vmem_specs(len(results)),
        out_shape=[
            jax.ShapeDtypeStruct((rows, PLANE * channels), dtype) for rows, dtype in results
        ],
        cost_estimate=took(2),
        name="unpack",
    )(x, *late)


def rim_before(x):
    count = lax.axis_size("ctx")
    rows, channels = x.shape
    x = x.reshape(rows, count // PLANE, PLANE, channels // count)
    parts = []
    for q in range(PLANE):
        route = [(i - 1, i + q) for i in range(PLANE, count, PLANE)]
        parts.append(send(x[:, :, q].reshape(rows, channels // PLANE), route))
    return functools.reduce(jnp.add, parts)


def late_rows(early):
    count = lax.axis_size("ctx")
    return [
        send(early, [(i + q, i - 1) for i in range(PLANE, count, PLANE)]) for q in range(PLANE)
    ]


def own_channels(x):
    count = lax.axis_size("ctx")
    rows, channels = x.shape
    x = x.reshape(rows, count // PLANE, PLANE, channels // count)
    x = lax.dynamic_index_in_dim(x, lax.axis_index("ctx") % PLANE, 2, keepdims=False)
    return x.reshape(rows, channels // PLANE)


def line_blocks(x):
    planes = lax.axis_size("ctx") // PLANE
    return [send(x, line_route(-k)) if k else x for k in range(planes)]


def place_blocks(blocks, axis):
    planes = len(blocks)
    mine = lax.axis_index("ctx") // PLANE
    size = blocks[0].shape[axis]
    shape = list(blocks[0].shape)
    shape[axis] = planes * size
    out = jnp.zeros(shape, blocks[0].dtype)
    for k, block in enumerate(blocks):
        at = lax.rem(mine + k, planes) * size
        out = lax.dynamic_update_slice(out, block, (at, 0) if axis == 0 else (0, at))
    return out


def after(x, *earlier):
    return lax.optimization_barrier((x,) + earlier)[0]


def pick(x, at, axis=0):
    return lax.dynamic_index_in_dim(x, at, axis, keepdims=False)


def sum_plane(mine, received):
    mine = mine + received
    half = mine.astype(BF16)
    routes = [[(i, i ^ bits) for i in range(lax.axis_size("ctx"))] for bits in range(1, PLANE)]
    total = mine
    for route in routes:
        total = total + send(half, route).astype(F32)
    return total, swap_mp(total)


def by_halves(mine, other):
    core = lax.axis_index("mp")
    return jnp.where(
        core == 0, jnp.concatenate([mine, other], axis=1), jnp.concatenate([other, mine], axis=1)
    )


def fill_padded(moved, before, padded, columns):
    rows = padded.shape[0] // PLANE // 8 * 8
    padded[8 - before.shape[0] : 8, columns] = before[:, columns].astype(F32)
    for q in range(PLANE):
        padded[8 + q * rows : 8 + (q + 1) * rows, columns] = moved[q, :rows, columns].astype(F32)


def taps(padded, weight, bias, start, rows, columns):
    first = 8 - (CONV - 1) + start
    total = bias[:, columns]
    for k in range(CONV):
        total = total + weight[k : k + 1, columns] * padded[first + k : first + k + rows, columns]
    return total


def head_kernel(moved, before, weight, bias, act_out, padded):
    tokens, width = act_out.shape
    rows = tokens // PLANE
    for column in range(0, width, COLUMNS):
        columns = slice(column, column + COLUMNS)
        fill_padded(moved, before, padded, columns)
        for start in range(0, tokens, rows):
            value = taps(padded, weight, bias, start, rows, columns)
            act_out[start : start + rows, columns] = (value / (1.0 + jnp.exp(-value))).astype(BF16)


def conv_head(moved, before, weight, bias, rows):
    channels = moved.shape[2]
    operands = (moved, before, weight, bias)
    return pl.pallas_call(
        head_kernel,
        in_specs=vmem_specs(len(operands)),
        out_shape=jax.ShapeDtypeStruct((PLANE * rows, channels), BF16),
        out_specs=vmem_specs(1)[0],
        scratch_shapes=[pltpu.VMEM((PLANE * rows + 8, channels), F32)],
        compiler_params=pltpu.CompilerParams(vmem_limit_bytes=VMEM_SMALL),
        cost_estimate=took(4),
        name="conv_head",
    )(*operands)


def tail_kernel(
    core, mine, other, rows_proj, grad_act, moved, before, weight, bias, dt_parts,
    packed_out, sums_out, early_out, grad, padded, grad_proj,
):
    tokens, width = grad_act.shape
    rows = tokens // PLANE
    rim = CONV - 1
    join_halves(core, mine, other, grad_proj)
    dt_rows = packed_out.shape[1] - rows
    for q in range(PLANE):
        at = slice(q * dt_rows, (q + 1) * dt_rows)
        total = dt_parts[0, at, :].astype(F32)
        for z in range(1, dt_parts.shape[0]):
            total = total + dt_parts[z, at, :].astype(F32)
        packed_out[q, rows:, :] = total.astype(BF16)
    for column in range(0, width, COLUMNS):
        columns = slice(column, column + COLUMNS)
        fill_padded(moved, before, padded, columns)
        grad[:tokens, columns] = lax.dot_general(
            grad_proj[...], rows_proj[:, columns], (((0,), (0,)), ((), ())),
            preferred_element_type=F32,
        )
        grad[tokens:, columns] = jnp.zeros((8, COLUMNS), F32)
        sums = [jnp.zeros((8, COLUMNS), F32)] * (CONV + 1)
        fold = lambda x: functools.reduce(jnp.add, [x[r : r + 8] for r in range(0, x.shape[0], 8)])
        piece = rows // 4
        for start in range(0, tokens, piece):
            at = slice(start, start + piece)
            shifts = [
                padded[8 - rim + k + start : 8 - rim + k + start + piece, columns]
                for k in range(CONV)
            ]
            value = bias[:, columns]
            for k in range(CONV):
                value = value + weight[k : k + 1, columns] * shifts[k]
            s = 1.0 / (1.0 + jnp.exp(-value))
            now = (grad_act[at, columns] + grad[at, columns]) * (s * (1.0 + value * (1.0 - s)))
            grad[at, columns] = now
            for k in range(CONV):
                sums[k] = sums[k] + fold(now * shifts[k])
            sums[CONV] = sums[CONV] + fold(now)
        for k in range(CONV + 1):
            sums_out[k : k + 1, columns] = jnp.sum(sums[k], axis=0, keepdims=True)
        for start in range(0, tokens, piece):
            total = jnp.zeros((piece, COLUMNS), F32)
            for k in range(CONV):
                first = rim - k + start
                total = total + weight[k : k + 1, columns] * grad[first : first + piece, columns]
            to = start % rows
            packed_out[start // rows, to : to + piece, columns] = total.astype(BF16)
        early_out[: LAST - rim, columns] = jnp.zeros((LAST - rim, COLUMNS), F32)
        for j in range(rim):
            early = jnp.zeros((1, COLUMNS), F32)
            for k in range(j + 1):
                early = early + weight[k : k + 1, columns] * grad[j - k : j - k + 1, columns]
            early_out[LAST - rim + j : LAST - rim + j + 1, columns] = early


def conv_tail(core, mine, other, rows_proj, grad_act, moved, before, weight, bias, dt_parts):
    tokens, channels = grad_act.shape
    operands = (core, mine, other, rows_proj, grad_act, moved, before, weight, bias, dt_parts)
    return pl.pallas_call(
        tail_kernel,
        in_specs=[pl.BlockSpec(memory_space=pltpu.SMEM)] + vmem_specs(len(operands) - 1),
        out_shape=[
            jax.ShapeDtypeStruct(moved.shape, BF16),
            jax.ShapeDtypeStruct((CONV + 1, channels), F32),
            jax.ShapeDtypeStruct((LAST, channels), F32),
        ],
        scratch_shapes=[
            pltpu.VMEM((tokens + 8, channels), F32),
            pltpu.VMEM((tokens + 8, channels), F32),
            pltpu.VMEM((mine.shape[0], tokens), BF16),
        ],
        compiler_params=pltpu.CompilerParams(vmem_limit_bytes=VMEM_SMALL),
        cost_estimate=took(8),
        name="conv_tail",
    )(*operands)


def line_carries(state, adjoint, a_log):
    planes = lax.axis_size("ctx") // PLANE
    mine = lax.axis_index("ctx") // PLANE
    rates = -jnp.exp(a_log)
    parts = {}
    for k in range(1, planes):
        parts[k] = send(jnp.where(mine + k < planes, state, adjoint), line_route(k))
    entering = []
    for order, valid in (
        (range(planes - 1, 0, -1), lambda k: mine - k >= 0),
        (range(1, planes), lambda k: mine - k < 0),
    ):
        carry = jnp.zeros((STATE, state.shape[1]), F32)
        for k in order:
            new = jnp.exp(rates * parts[k][STATE:]) * carry + parts[k][:STATE]
            carry = jnp.where(valid(k), new, carry)
        entering.append(carry)
    return jnp.concatenate(entering, axis=0)


def sum_line(x):
    planes = lax.axis_size("ctx") // PLANE
    mine = lax.axis_index("ctx") // PLANE
    x = x.reshape(x.shape[0], planes, x.shape[1] // planes)
    total = pick(x, mine, 1)
    for k in range(1, planes):
        total = total + send(pick(x, lax.rem(mine + k, planes), 1), line_route(k))
    return total


def silu_parts(x):
    s = jax.nn.sigmoid(x)
    return x * s, s * (1.0 + x * (1.0 - s))


def conv_forward(padded, weight, bias, length):
    pre_act = jnp.zeros((length, padded.shape[1]), F32) + bias
    for k in range(CONV):
        pre_act = pre_act + weight[k][None, :] * padded[k : k + length]
    return pre_act


def conv_backward(grad_padded, weight, length):
    grad = jnp.zeros((length, grad_padded.shape[1]), F32)
    for k in range(CONV):
        grad = grad + weight[k][None, :] * grad_padded[CONV - 1 - k : CONV - 1 - k + length]
    return grad.astype(BF16)


def conv_sums(grad, padded):
    length = grad.shape[0]
    return jnp.stack(
        [jnp.sum(grad * padded[k : k + length], axis=0) for k in range(CONV)]
        + [jnp.sum(grad, axis=0)]
    )


def matmul(x, y, dims):
    return lax.dot_general(x, y, ((dims[:1], dims[1:]), ((), ())), preferred_element_type=F32)


def gate_parts(gate_in, upstream, forget_flags):
    grad_out = -forget_flags.astype(F32)[:, None] * upstream.astype(F32)
    value, slope = silu_parts(gate_in.astype(F32))
    return (grad_out * value).astype(BF16), grad_out * slope


def outputs(grad_seq, grad_gate, grad_dtw, sums):
    return (
        grad_seq, grad_gate, grad_dtw,
        sums[:CONV], sums[CONV], sums[CONV + 1], sums[CONV + 3 :], sums[CONV + 2],
    )


def plane_body(
    seq_in, gate_in, upstream, forget_flags, conv_weight, conv_bias,
    proj_weight, dt_weight, dt_bias, a_log, skip_gain,
):
    rim = CONV - 1
    core = lax.axis_index("mp")
    planes = lax.axis_size("ctx") // PLANE
    here = core.astype(jnp.int32).reshape(1)
    rows, dt_rows = seq_in.shape[0], dt_weight.shape[0]
    half = PLANE * rows // 2
    packed = by_owner(seq_in, dt_weight)
    proj_blocks = line_blocks(proj_weight.T)
    moved = in_plane(packed)
    before = rim_before(seq_in[rows - rim :])
    weight, bias, step_bias, rates, gain = (
        own_channels(x)
        for x in (conv_weight, conv_bias[None], dt_bias[None], a_log, skip_gain[None])
    )
    act = conv_head(moved, before, weight, bias, rows)
    dt_plane = moved[:, rows:].reshape(PLANE * dt_rows, -1)
    grad_mixed, _ = gate_parts(gate_in, upstream, forget_flags)
    mixed_packed = by_owner(grad_mixed)
    grad_mixed = in_plane(after(mixed_packed, moved)).reshape(PLANE * rows, -1)

    proj_blocks = after(tuple(proj_blocks), act, mixed_packed, dt_plane)
    rows_proj = place_blocks(proj_blocks, 1)
    dt_blocks = line_blocks(dt_plane)
    part = lambda at: matmul(rows_proj, lax.dynamic_slice_in_dim(act, at * half, half), (1, 1))
    mine, other = sum_plane(part(core), swap_mp(part(1 - core)))
    rows_dt = place_blocks(dt_blocks, 0)
    step, sig, state, adjoint, bc = scan_local(
        here, mine, other, rows_dt, step_bias, act, grad_mixed, rates
    )
    low = by_halves(mine[:RANK].astype(BF16), other[:RANK].astype(BF16))
    carries = line_carries(state, adjoint, rates)
    mixed, grad_pre, grad_act, grad_rate, grad_vecs, grad_mine, grad_other = scan_full(
        here, bc, rows_dt, step, sig, act, grad_mixed, rates, carries, gain
    )

    dtw_sums = matmul(low, grad_pre, (1, 0)).astype(BF16)
    dtw_moved = along_line(dtw_sums.reshape(planes, RANK // planes, -1))
    mine, other = sum_plane(grad_mine, swap_mp(after(grad_other, dtw_sums)))
    mine, other = mine.astype(BF16), other.astype(BF16)
    packed, grad_conv, early = conv_tail(
        here, mine, other, rows_proj, grad_act, moved, before, weight, bias, dtw_moved
    )
    grad_gate = in_plane(after(mixed, mine).reshape(PLANE, rows, -1))
    returned = in_plane(after(packed, grad_gate))
    grad_gate = gate_gradient(after(grad_gate, packed), gate_in, upstream, forget_flags)
    late = late_rows(after(early, grad_gate))
    sums = jnp.concatenate([grad_conv, grad_vecs, grad_rate], axis=0)
    sums = sum_line(after(sums, grad_gate))
    grad_seq, grad_dtw = to_tokens(returned, (rows, BF16), (dt_rows, F32), late=late)
    return outputs(grad_seq, grad_gate, grad_dtw, sums)


def block_body(
    seq_in, gate_in, upstream, forget_flags, conv_weight, conv_bias,
    proj_weight, dt_weight, dt_bias, a_log, skip_gain,
):
    length = seq_in.shape[0]
    rim = CONV - 1
    padded = jnp.concatenate([shifted(seq_in[length - rim :], "ctx", 1), seq_in], axis=0)
    pre_act = conv_forward(padded, conv_weight, conv_bias[None], length)
    act = jax.nn.silu(pre_act).astype(BF16)
    rows_proj = lax.all_gather(proj_weight, "ctx", axis=0, tiled=True)
    rows_dt = lax.all_gather(dt_weight, "ctx", axis=0, tiled=True)
    projected = lax.psum(matmul(rows_proj, act, (0, 1)), "mp")
    low = projected[:RANK].astype(BF16)
    halves = (jnp.zeros((1,), jnp.int32), projected[:, : length // 2], projected[:, length // 2 :])
    grad_mixed, gate_factor = gate_parts(gate_in, upstream, forget_flags)
    step, sig, state, adjoint, bc = scan_local(
        *halves, rows_dt, dt_bias[None], act, grad_mixed, a_log
    )
    carries = exchange_carries(jnp.concatenate([state[:STATE], adjoint], axis=0), a_log)
    mixed, grad_pre, grad_act, grad_rate, grad_vecs, first, second = scan_full(
        halves[0], bc, rows_dt, step, sig, act, grad_mixed, a_log, carries, skip_gain[None]
    )
    grad_gate = (gate_factor * mixed.astype(F32)).astype(BF16)
    grad_proj = lax.psum(jnp.concatenate([first, second], axis=1), "mp").astype(BF16)
    grad_pre_act = (grad_act + matmul(grad_proj, rows_proj, (0, 1))) * silu_parts(pre_act)[1]
    grad_padded = jnp.concatenate([grad_pre_act, shifted(grad_pre_act[:rim], "ctx", -1)], axis=0)
    grad_seq = conv_backward(grad_padded, conv_weight, length)
    scatter = lambda x, axis: lax.psum_scatter(x, "ctx", scatter_dimension=axis, tiled=True)
    grad_dtw = scatter(matmul(low, grad_pre, (1, 0)), 0)
    sums = scatter(
        jnp.concatenate([conv_sums(grad_pre_act, padded), grad_vecs, grad_rate], axis=0), 1
    )
    return outputs(grad_seq, grad_gate, grad_dtw, sums)


def solution(mesh):
    shares = mesh.shape["mp"] == 2 and mesh.shape["ctx"] in (8, 16)
    body = plane_body if shares else block_body
    return jax.shard_map(
        body,
        mesh=mesh,
        in_specs=(
            P("ctx", "mp"),
            P("ctx", "mp"),
            P("ctx", "mp"),
            P("ctx"),
            P(None, "mp"),
            P("mp"),
            P(("mp", "ctx"), None),
            P("ctx", "mp"),
            P("mp"),
            P(None, "mp"),
            P("mp"),
        ),
        out_specs=(
            P("ctx", "mp"),
            P("ctx", "mp"),
            P("ctx", "mp"),
            P(None, ("mp", "ctx")),
            P(("mp", "ctx")),
            P(("mp", "ctx")),
            P(None, ("mp", "ctx")),
            P(("mp", "ctx")),
        ),
        check_vma=False,
    )
```

```python
import functools
import jax
import jax.numpy as jnp
from jax import lax
from jax.experimental import pallas as pl
from jax.experimental.pallas import tpu as pltpu
from jax.sharding import PartitionSpec as P

STATE = 16
RANK = 512
CONV = 4
PLANE = 4
LANES = 128
GROUP = 8
UNROLL = 16
BLOCK = 32
COLUMNS = 256
LAST = 16
LOG2E = 1.4426950408889634
LN2 = 0.6931471805599453
VMEM_LIMIT = 58 * 1024 * 1024
VMEM_SMALL = 24 * 1024 * 1024
F32 = jnp.float32
BF16 = jnp.bfloat16


def row_sums(parts):
    parts = [
        functools.reduce(jnp.add, [p[r : r + 8] for r in range(0, p.shape[0], 8)]) for p in parts
    ]
    row = lax.broadcasted_iota(jnp.int32, (8, LANES), 0)
    low = row < 4
    halves = [
        jnp.where(low, parts[k], parts[k + 4])
        + pltpu.roll(jnp.where(low, parts[k + 4], parts[k]), 4, 0)
        for k in range(4)
    ]
    second = (row & 2) == 0
    quarters = [
        jnp.where(
            second,
            halves[k] + pltpu.roll(halves[k], 6, 0),
            halves[k + 2] + pltpu.roll(halves[k + 2], 2, 0),
        )
        for k in range(2)
    ]
    return jnp.where(
        (row & 1) == 0,
        quarters[0] + pltpu.roll(quarters[0], 7, 0),
        quarters[1] + pltpu.roll(quarters[1], 1, 0),
    )


def join_halves(core, mine, other, out):
    half = mine.shape[1]
    for which, (first, second) in enumerate(((mine, other), (other, mine))):

        @pl.when(core[0] == which)
        def _():
            out[:, :half] = first[...].astype(out.dtype)
            out[:, half:] = second[...].astype(out.dtype)


def spread_rows(bc, out):
    values = bc[...].T
    high = values.astype(BF16)
    rest = values - high.astype(F32)
    middle = rest.astype(BF16)
    lowest = (rest - middle.astype(F32)).astype(BF16)
    parts = jnp.concatenate([high, middle, lowest], axis=1)
    count = bc.shape[0]
    column = lax.broadcasted_iota(jnp.int32, (3 * count, LANES), 0) % count
    for n in range(count):
        pick_n = jnp.where(column == n, 1.0, 0.0).astype(BF16)
        out[n] = jnp.dot(parts, pick_n, preferred_element_type=F32)


def local_kernel(
    core, mine, other, dtw, dtb, act, g, alog, step_to, sig_to, state_out, adjoint_out, bc,
    a2, us, gs, spread, low, step_out, sig_out, done,
):
    tokens, width = act.shape
    rank = dtw.shape[0]
    join_halves(core, mine.at[:rank], other.at[:rank], low)
    join_halves(core, mine.at[rank:], other.at[rank:], bc)
    spread_rows(bc, spread)
    rows = width // LANES
    block = min(tokens, BLOCK)
    a2[...] = (-LOG2E * jnp.exp(alog[...])).reshape(STATE, rows, LANES)

    for column in range(0, width, 256):
        columns = slice(column, column + 256)
        sig_out[:, columns] = lax.dot_general(
            low[...], dtw[:, columns], (((0,), (0,)), ((), ())), preferred_element_type=F32
        )

    def prepare(i, total):
        at = pl.ds(pl.multiple_of(i * block, block), block)
        pre = sig_out[at, :] + dtb[...]
        tail = jnp.exp(-jnp.abs(pre))
        step = jnp.maximum(pre, 0.0) + jnp.log1p(tail)
        sig_out[at, :] = jnp.where(pre >= 0.0, 1.0, tail) / (1.0 + tail)
        step_out[at] = step.reshape(block, rows, LANES)
        us[at] = (step * act[at, :].astype(F32)).reshape(block, rows, LANES)
        gs[at] = g[at, :].astype(F32).reshape(block, rows, LANES)
        return total + jnp.sum(step, axis=0, keepdims=True)

    total = lax.fori_loop(0, tokens // block, prepare, jnp.zeros((1, width), F32))
    copies = [
        pltpu.make_async_copy(step_out, step_to, done.at[0]),
        pltpu.make_async_copy(sig_out, sig_to, done.at[1]),
    ]
    for copy in copies:
        copy.start()
    state_out[STATE : STATE + 1, :] = total
    adjoint_out[STATE : STATE + 1, :] = total
    zeros = jnp.zeros((8, LANES), F32)
    ones = jnp.ones((8, LANES), F32)
    for r in range(0, rows, 8):
        part = slice(r, r + 8)
        for base in range(0, STATE, GROUP):

            def move(t, carry):
                h, p, lam = carry
                s, u, g_now = step_out[t, part, :], us[t, part, :], gs[t, part, :]
                h, p, lam = list(h), list(p), list(lam)
                for k in range(GROUP):
                    n = base + k
                    d = jnp.exp2(s * a2[n, part, :])
                    h[k] = d * h[k] + spread[n, pl.ds(t, 1), :] * u
                    p[k] = d * p[k]
                    lam[k] = lam[k] + (spread[STATE + n, pl.ds(t, 1), :] * g_now) * p[k]
                return tuple(h), tuple(p), tuple(lam)

            h, _, lam = lax.fori_loop(
                0, tokens, move, ((zeros,) * GROUP, (ones,) * GROUP, (zeros,) * GROUP),
                unroll=UNROLL,
            )
            columns = slice(r * LANES, (r + 8) * LANES)
            for k in range(GROUP):
                n = base + k
                state_out[n : n + 1, columns] = h[k].reshape(1, 8 * LANES)
                adjoint_out[n : n + 1, columns] = lam[k].reshape(1, 8 * LANES)
    for copy in copies:
        copy.wait()


def full_kernel(
    core, bc, dtw, step, sig, act, g, alog, carries, skip,
    mixed_out, pre_out, act_out, rate_out, vec_out, mine_out, other_out,
    a2, acts, gs, hist, mixed, s1, s2, gb, gc, spread, both_rows,
):
    tokens, rows, _ = step.shape
    width = rows * LANES
    rank = dtw.shape[0]
    spread_rows(bc, spread)
    block = min(tokens, BLOCK)
    dense, flat = (block, rows, LANES), (block, width)
    a2[...] = (-LOG2E * jnp.exp(alog[...])).reshape(STATE, rows, LANES)

    @pl.loop(0, tokens // block)
    def _(i):
        at = pl.ds(pl.multiple_of(i * block, block), block)
        acts[at] = act[at, :].astype(F32).reshape(dense)
        gs[at] = g[at, :].astype(F32).reshape(dense)

    carry_dense = carries[...].reshape(2 * STATE, rows, LANES)
    skip_dense = skip[...].reshape(rows, LANES)
    zero = jnp.zeros((rows, LANES), F32)

    for base in range(0, STATE, GROUP):
        group = slice(base, base + GROUP)

        def forward(t, h):
            s = step[t]
            u = s * acts[t]
            g_now = gs[t]
            h = list(h)
            total = skip_dense * acts[t] if base == 0 else mixed[t]
            for k in range(GROUP):
                n = base + k
                d = jnp.exp2(s * a2[n])
                h[k] = d * h[k] + spread[n, pl.ds(t, 1), :] * u
                hist[t + 1, k] = h[k]
                total = total + spread[STATE + n, pl.ds(t, 1), :] * h[k]
            mixed[t] = total
            gc[t, group, :] = row_sums([g_now * part for part in h])
            return tuple(h)

        hist[0] = carry_dense[group]
        lax.fori_loop(
            0, tokens, forward, tuple(carry_dense[base + k] for k in range(GROUP)), unroll=UNROLL
        )

        def backward(i, carry):
            m, ga = carry
            m, ga = list(m), list(ga)
            t = tokens - 1 - i
            s = step[t]
            u = s * acts[t]
            g_now = gs[t]
            total1 = zero if base == 0 else s1[t]
            total2 = zero if base == 0 else s2[t]
            products = []
            for k in range(GROUP):
                n = base + k
                lam = spread[STATE + n, pl.ds(t, 1), :] * g_now + m[k]
                total1 = total1 + spread[n, pl.ds(t, 1), :] * lam
                products.append(lam * u)
                m[k] = jnp.exp2(s * a2[n]) * lam
                q = m[k] * hist[t, k]
                total2 = total2 + q * a2[n]
                ga[k] = ga[k] + q * s
            gb[t, group, :] = row_sums(products)
            s1[t] = total1
            s2[t] = total2
            return tuple(m), tuple(ga)

        _, ga = lax.fori_loop(
            0, tokens, backward,
            (tuple(carry_dense[STATE + base + k] for k in range(GROUP)), (zero,) * GROUP),
            unroll=UNROLL,
        )
        for k in range(GROUP):
            n = base + k
            rate_out[n : n + 1, :] = (LN2 * a2[n] * ga[k]).reshape(1, width)

    lane = lax.broadcasted_iota(jnp.int32, (1, STATE, LANES), 2)
    state = lax.broadcasted_iota(jnp.int32, (1, STATE, LANES), 1)
    ones = jnp.ones((LANES, LANES), BF16)

    def finish(i, totals):
        at = pl.ds(pl.multiple_of(i * block, block), block)
        first, act_now, g_now = s1[at], acts[at], gs[at]
        mixed_out[at, :] = mixed[at].reshape(flat).astype(BF16)
        grad_pre = (LN2 * s2[at] + first * act_now).reshape(flat) * sig[at, :]
        pre_out[at, :] = grad_pre.astype(BF16)
        act_out[at, :] = (first * step[at] + skip_dense[None] * g_now).reshape(flat)
        both = jnp.zeros((block, LANES), F32)
        for offset, ref in ((0, gb), (STATE, gc)):
            sums = jnp.dot(
                ref[at].reshape(block * STATE, LANES).astype(BF16), ones,
                preferred_element_type=F32,
            ).reshape(block, STATE, LANES)
            both = both + jnp.sum(jnp.where(lane == state + offset, sums, 0.0), axis=1)
        both_rows[at, :] = both
        return (
            totals[0] + jnp.sum(grad_pre, axis=0, keepdims=True),
            totals[1] + jnp.sum(g_now * act_now, axis=0),
        )

    bias, gain = lax.fori_loop(
        0, tokens // block, finish, (jnp.zeros((1, width), F32), zero)
    )
    vec_out[0:1, :] = bias
    vec_out[1:2, :] = gain.reshape(1, width)
    half = tokens // 2
    for which, out in ((core[0], mine_out), (1 - core[0], other_out)):
        at = pl.ds(pl.multiple_of(which * half, half), half)
        out[:rank, :] = lax.dot_general(
            dtw[...], pre_out[at, :], (((1,), (1,)), ((), ())), preferred_element_type=F32
        ).astype(out.dtype)
        out[rank:, :] = both_rows[at, :].T[: 2 * STATE].astype(out.dtype)


def took(microseconds):
    return pl.CostEstimate(
        flops=0, bytes_accessed=int(microseconds * 3.6e6), transcendentals=0
    )


def vmem_specs(count):
    return [pl.BlockSpec(memory_space=pltpu.VMEM)] * count


def scan_local(core, mine, other, dtw, dtb, act, g, alog):
    tokens, channels = act.shape
    dense = (tokens, channels // LANES, LANES)
    operands = (core, mine, other, dtw, dtb, act, g, alog)
    ends = jax.ShapeDtypeStruct((STATE + 1, channels), F32)
    return pl.pallas_call(
        local_kernel,
        in_specs=[pl.BlockSpec(memory_space=pltpu.SMEM)] + vmem_specs(len(operands) - 1),
        out_shape=[
            jax.ShapeDtypeStruct(dense, F32), jax.ShapeDtypeStruct((tokens, channels), F32), ends, ends,
            jax.ShapeDtypeStruct((2 * STATE, tokens), F32),
        ],
        out_specs=[pl.BlockSpec(memory_space=pl.ANY)] * 2 + vmem_specs(3),
        scratch_shapes=[
            pltpu.VMEM((STATE,) + dense[1:], F32), pltpu.VMEM(dense, F32), pltpu.VMEM(dense, F32),
            pltpu.VMEM((2 * STATE, tokens, LANES), F32), pltpu.VMEM((dtw.shape[0], tokens), BF16),
            pltpu.VMEM(dense, F32), pltpu.VMEM((tokens, channels), F32),
            pltpu.SemaphoreType.DMA((2,)),
        ],
        compiler_params=pltpu.CompilerParams(vmem_limit_bytes=VMEM_LIMIT),
        cost_estimate=took(22),
        name="scan_local",
    )(*operands)


def scan_full(core, bc, dtw, step, sig, act, g, alog, carries, skip):
    tokens, channels = act.shape
    dense = (tokens, channels // LANES, LANES)
    flat = (tokens, channels)
    operands = (core, bc, dtw, step, sig, act, g, alog, carries, skip)
    small = pltpu.VMEM((tokens, STATE, LANES), F32)
    half = (dtw.shape[0] + 2 * STATE, tokens // 2)
    return pl.pallas_call(
        full_kernel,
        in_specs=[pl.BlockSpec(memory_space=pltpu.SMEM)] + vmem_specs(len(operands) - 1),
        out_shape=[
            jax.ShapeDtypeStruct(flat, BF16),
            jax.ShapeDtypeStruct(flat, BF16),
            jax.ShapeDtypeStruct(flat, F32),
            jax.ShapeDtypeStruct((STATE, channels), F32),
            jax.ShapeDtypeStruct((2, channels), F32),
            jax.ShapeDtypeStruct(half, F32),
            jax.ShapeDtypeStruct(half, BF16),
        ],
        scratch_shapes=[
            pltpu.VMEM((STATE,) + dense[1:], F32),
            pltpu.VMEM(dense, F32),
            pltpu.VMEM(dense, F32),
            pltpu.VMEM((tokens + 1, GROUP) + dense[1:], F32),
            pltpu.VMEM(dense, F32),
            pltpu.VMEM(dense, F32),
            pltpu.VMEM(dense, F32),
            small,
            small,
            pltpu.VMEM((2 * STATE, tokens, LANES), F32),
            pltpu.VMEM((tokens, LANES), F32),
        ],
        compiler_params=pltpu.CompilerParams(vmem_limit_bytes=VMEM_LIMIT),
        cost_estimate=took(51),
        name="scan_full",
    )(*operands)


def carry_kernel(ends, alog, out):
    count = ends.shape[0]
    a2 = -LOG2E * jnp.exp(alog[...])
    h = jnp.zeros(a2.shape, F32)
    for j in range(count):
        out[j, :STATE, :] = h
        decay = jnp.exp2(a2 * ends[j, 2 * STATE : 2 * STATE + 1, :])
        h = decay * h + ends[j, :STATE, :]
    lam = jnp.zeros(a2.shape, F32)
    for j in reversed(range(count)):
        out[j, STATE:, :] = lam
        decay = jnp.exp2(a2 * ends[j, 2 * STATE : 2 * STATE + 1, :])
        lam = decay * lam + ends[j, STATE : 2 * STATE, :]


def exchange_carries(ends, a_log):
    count, mine = lax.axis_size("ctx"), lax.axis_index("ctx")
    rows, channels = ends.shape
    width = channels // count
    parts = lax.all_to_all(
        ends.reshape(rows, count, width).transpose(1, 0, 2), "ctx", 0, 0, tiled=True
    )
    own_rates = lax.dynamic_slice_in_dim(a_log, mine * width, width, axis=1)
    carried = pl.pallas_call(
        carry_kernel,
        out_shape=jax.ShapeDtypeStruct((count, 2 * STATE, width), F32),
        name="carry",
    )(parts, own_rates)
    back = lax.all_to_all(carried, "ctx", 0, 0, tiled=True)
    return back.transpose(1, 0, 2).reshape(2 * STATE, channels)


def shifted(block, axis, distance):
    devices = range(lax.axis_size(axis))
    route = [(i - distance, i) for i in devices if i - distance in devices]
    return lax.ppermute(block, axis, route)


def send(x, route, dtype=None):
    if dtype is None:
        return lax.ppermute(x, "ctx", route)
    return lax.ppermute(x.astype(dtype), "ctx", route).astype(x.dtype)


def flip_route(bit):
    return [(i, i ^ bit) for i in range(lax.axis_size("ctx"))]


def line_route(k):
    count = lax.axis_size("ctx")
    return [(i, (i + PLANE * k) % count) for i in range(count)]


def swap_mp(x):
    return lax.ppermute(x, "mp", [(0, 1), (1, 0)])


def plane_groups():
    count = lax.axis_size("ctx")
    return [list(range(i, i + PLANE)) for i in range(0, count, PLANE)]


def in_plane(x):
    return lax.all_to_all(x, "ctx", 0, 0, axis_index_groups=plane_groups(), tiled=True)


def pack_kernel(share, *refs):
    *inputs, out = refs
    row = 0
    for x in inputs:
        rows = slice(row, row + x.shape[0])
        row += x.shape[0]
        for q in range(PLANE):
            for z in range(out.shape[2] // share):
                source = (z * PLANE + q) * share
                out[q, rows, z * share : (z + 1) * share] = x[:, source : source + share]


def unpack_kernel(share, count, x, *refs):
    late, outs = refs[:-count], refs[-count:]
    row = 0
    for at, out in enumerate(outs):
        rows = slice(row, row + out.shape[0])
        row += out.shape[0]
        for q in range(PLANE):
            for z in range(x.shape[2] // share):
                source = slice(z * share, (z + 1) * share)
                target = (z * PLANE + q) * share
                target = slice(target, target + share)
                out[:, target] = x[q, rows, source].astype(out.dtype)
                if late and at == 0:
                    last = slice(out.shape[0] - LAST, out.shape[0])
                    total = x[q, last, source].astype(F32) + late[q][:, source]
                    out[last, target] = total.astype(out.dtype)


def gate_kernel(share, x, gate, up, flags, out):
    for q in range(PLANE):
        for z in range(x.shape[2] // share):
            target = (z * PLANE + q) * share
            target = slice(target, target + share)
            value = gate[:, target].astype(F32)
            s = 1.0 / (1.0 + jnp.exp(-value))
            factor = -flags[...] * up[:, target].astype(F32) * (s * (1.0 + value * (1.0 - s)))
            mixed = x[q, :, z * share : (z + 1) * share].astype(F32)
            out[:, target] = (factor * mixed).astype(BF16)


def gate_gradient(x, gate, up, flags):
    share = x.shape[2] * PLANE // lax.axis_size("ctx")
    return pl.pallas_call(
        functools.partial(gate_kernel, share),
        in_specs=vmem_specs(4),
        out_specs=vmem_specs(1)[0],
        out_shape=jax.ShapeDtypeStruct(gate.shape, BF16),
        cost_estimate=took(4),
        name="gate_gradient",
    )(x, gate, up, flags.astype(F32)[:, None])


def along_line(x):
    count = lax.axis_size("ctx")
    groups = [list(range(i, count, PLANE)) for i in range(PLANE)]
    return lax.all_to_all(x, "ctx", 0, 0, axis_index_groups=groups, tiled=True)


def by_owner(*arrays):
    channels = arrays[0].shape[1]
    rows = sum(x.shape[0] for x in arrays)
    share = channels // lax.axis_size("ctx")
    return pl.pallas_call(
        functools.partial(pack_kernel, share),
        in_specs=vmem_specs(len(arrays)),
        out_specs=vmem_specs(1)[0],
        out_shape=jax.ShapeDtypeStruct((PLANE, rows, channels // PLANE), arrays[0].dtype),
        cost_estimate=took(2),
        name="pack",
    )(*arrays)


def to_tokens(x, *results, late=()):
    channels = x.shape[2]
    share = channels * PLANE // lax.axis_size("ctx")
    return pl.pallas_call(
        functools.partial(unpack_kernel, share, len(results)),
        in_specs=vmem_specs(1 + len(late)),
        out_specs=vmem_specs(len(results)),
        out_shape=[
            jax.ShapeDtypeStruct((rows, PLANE * channels), dtype) for rows, dtype in results
        ],
        cost_estimate=took(2),
        name="unpack",
    )(x, *late)


def rim_before(x):
    count = lax.axis_size("ctx")
    rows, channels = x.shape
    x = x.reshape(rows, count // PLANE, PLANE, channels // count)
    parts = []
    for q in range(PLANE):
        route = [(i - 1, i + q) for i in range(PLANE, count, PLANE)]
        parts.append(send(x[:, :, q].reshape(rows, channels // PLANE), route))
    return functools.reduce(jnp.add, parts)


def late_rows(early):
    count = lax.axis_size("ctx")
    return [
        send(early, [(i + q, i - 1) for i in range(PLANE, count, PLANE)]) for q in range(PLANE)
    ]


def own_channels(x):
    count = lax.axis_size("ctx")
    rows, channels = x.shape
    x = x.reshape(rows, count // PLANE, PLANE, channels // count)
    x = lax.dynamic_index_in_dim(x, lax.axis_index("ctx") % PLANE, 2, keepdims=False)
    return x.reshape(rows, channels // PLANE)


def line_blocks(x):
    planes = lax.axis_size("ctx") // PLANE
    return [send(x, line_route(-k)) if k else x for k in range(planes)]


def place_blocks(blocks, axis):
    planes = len(blocks)
    mine = lax.axis_index("ctx") // PLANE
    size = blocks[0].shape[axis]
    shape = list(blocks[0].shape)
    shape[axis] = planes * size
    out = jnp.zeros(shape, blocks[0].dtype)
    for k, block in enumerate(blocks):
        at = lax.rem(mine + k, planes) * size
        out = lax.dynamic_update_slice(out, block, (at, 0) if axis == 0 else (0, at))
    return out


def after(x, *earlier):
    return lax.optimization_barrier((x,) + earlier)[0]


def pick(x, at, axis=0):
    return lax.dynamic_index_in_dim(x, at, axis, keepdims=False)


def sum_plane(mine, received):
    mine = mine + received.astype(F32)
    half = mine.astype(BF16)
    routes = [[(i, i ^ bits) for i in range(lax.axis_size("ctx"))] for bits in range(1, PLANE)]
    total = mine
    for route in routes:
        total = total + send(half, route).astype(F32)
    return total, swap_mp(total)


def by_halves(mine, other):
    core = lax.axis_index("mp")
    return jnp.where(
        core == 0, jnp.concatenate([mine, other], axis=1), jnp.concatenate([other, mine], axis=1)
    )


def fill_padded(moved, before, padded, columns):
    rows = padded.shape[0] // PLANE // 8 * 8
    padded[8 - before.shape[0] : 8, columns] = before[:, columns].astype(F32)
    for q in range(PLANE):
        padded[8 + q * rows : 8 + (q + 1) * rows, columns] = moved[q, :rows, columns].astype(F32)


def taps(padded, weight, bias, start, rows, columns):
    first = 8 - (CONV - 1) + start
    total = bias[:, columns]
    for k in range(CONV):
        total = total + weight[k : k + 1, columns] * padded[first + k : first + k + rows, columns]
    return total


def head_kernel(moved, before, weight, bias, act_out, padded):
    tokens, width = act_out.shape
    rows = tokens // PLANE
    for column in range(0, width, COLUMNS):
        columns = slice(column, column + COLUMNS)
        fill_padded(moved, before, padded, columns)
        for start in range(0, tokens, rows):
            value = taps(padded, weight, bias, start, rows, columns)
            act_out[start : start + rows, columns] = (value / (1.0 + jnp.exp(-value))).astype(BF16)


def conv_head(moved, before, weight, bias, rows):
    channels = moved.shape[2]
    operands = (moved, before, weight, bias)
    return pl.pallas_call(
        head_kernel,
        in_specs=vmem_specs(len(operands)),
        out_shape=jax.ShapeDtypeStruct((PLANE * rows, channels), BF16),
        out_specs=vmem_specs(1)[0],
        scratch_shapes=[pltpu.VMEM((PLANE * rows + 8, channels), F32)],
        compiler_params=pltpu.CompilerParams(vmem_limit_bytes=VMEM_SMALL),
        cost_estimate=took(4),
        name="conv_head",
    )(*operands)


def tail_kernel(
    core, mine, other, rows_proj, grad_act, moved, before, weight, bias, dt_parts,
    packed_out, sums_out, early_out, grad, padded, grad_proj,
):
    tokens, width = grad_act.shape
    rows = tokens // PLANE
    rim = CONV - 1
    join_halves(core, mine, other, grad_proj)
    dt_rows = packed_out.shape[1] - rows
    for q in range(PLANE):
        at = slice(q * dt_rows, (q + 1) * dt_rows)
        total = dt_parts[0, at, :].astype(F32)
        for z in range(1, dt_parts.shape[0]):
            total = total + dt_parts[z, at, :].astype(F32)
        packed_out[q, rows:, :] = total.astype(BF16)
    for column in range(0, width, COLUMNS):
        columns = slice(column, column + COLUMNS)
        fill_padded(moved, before, padded, columns)
        grad[:tokens, columns] = lax.dot_general(
            grad_proj[...], rows_proj[:, columns], (((0,), (0,)), ((), ())),
            preferred_element_type=F32,
        )
        grad[tokens:, columns] = jnp.zeros((8, COLUMNS), F32)
        sums = [jnp.zeros((8, COLUMNS), F32)] * (CONV + 1)
        fold = lambda x: functools.reduce(jnp.add, [x[r : r + 8] for r in range(0, x.shape[0], 8)])
        piece = rows // 4
        for start in range(0, tokens, piece):
            at = slice(start, start + piece)
            shifts = [
                padded[8 - rim + k + start : 8 - rim + k + start + piece, columns]
                for k in range(CONV)
            ]
            value = bias[:, columns]
            for k in range(CONV):
                value = value + weight[k : k + 1, columns] * shifts[k]
            s = 1.0 / (1.0 + jnp.exp(-value))
            now = (grad_act[at, columns] + grad[at, columns]) * (s * (1.0 + value * (1.0 - s)))
            grad[at, columns] = now
            for k in range(CONV):
                sums[k] = sums[k] + fold(now * shifts[k])
            sums[CONV] = sums[CONV] + fold(now)
        for k in range(CONV + 1):
            sums_out[k : k + 1, columns] = jnp.sum(sums[k], axis=0, keepdims=True)
        for start in range(0, tokens, piece):
            total = jnp.zeros((piece, COLUMNS), F32)
            for k in range(CONV):
                first = rim - k + start
                total = total + weight[k : k + 1, columns] * grad[first : first + piece, columns]
            to = start % rows
            packed_out[start // rows, to : to + piece, columns] = total.astype(BF16)
        early_out[: LAST - rim, columns] = jnp.zeros((LAST - rim, COLUMNS), F32)
        for j in range(rim):
            early = jnp.zeros((1, COLUMNS), F32)
            for k in range(j + 1):
                early = early + weight[k : k + 1, columns] * grad[j - k : j - k + 1, columns]
            early_out[LAST - rim + j : LAST - rim + j + 1, columns] = early


def conv_tail(core, mine, other, rows_proj, grad_act, moved, before, weight, bias, dt_parts):
    tokens, channels = grad_act.shape
    operands = (core, mine, other, rows_proj, grad_act, moved, before, weight, bias, dt_parts)
    return pl.pallas_call(
        tail_kernel,
        in_specs=[pl.BlockSpec(memory_space=pltpu.SMEM)] + vmem_specs(len(operands) - 1),
        out_shape=[
            jax.ShapeDtypeStruct(moved.shape, BF16),
            jax.ShapeDtypeStruct((CONV + 1, channels), F32),
            jax.ShapeDtypeStruct((LAST, channels), F32),
        ],
        scratch_shapes=[
            pltpu.VMEM((tokens + 8, channels), F32),
            pltpu.VMEM((tokens + 8, channels), F32),
            pltpu.VMEM((mine.shape[0], tokens), BF16),
        ],
        compiler_params=pltpu.CompilerParams(vmem_limit_bytes=VMEM_SMALL),
        cost_estimate=took(8),
        name="conv_tail",
    )(*operands)


def line_carries(state, adjoint, a_log):
    planes = lax.axis_size("ctx") // PLANE
    mine = lax.axis_index("ctx") // PLANE
    rates = -jnp.exp(a_log)
    parts = {}
    for k in range(1, planes):
        parts[k] = send(jnp.where(mine + k < planes, state, adjoint), line_route(k))
    entering = []
    for order, valid in (
        (range(planes - 1, 0, -1), lambda k: mine - k >= 0),
        (range(1, planes), lambda k: mine - k < 0),
    ):
        carry = jnp.zeros((STATE, state.shape[1]), F32)
        for k in order:
            new = jnp.exp(rates * parts[k][STATE:]) * carry + parts[k][:STATE]
            carry = jnp.where(valid(k), new, carry)
        entering.append(carry)
    return jnp.concatenate(entering, axis=0)


def sum_line(x):
    planes = lax.axis_size("ctx") // PLANE
    mine = lax.axis_index("ctx") // PLANE
    x = x.reshape(x.shape[0], planes, x.shape[1] // planes)
    total = pick(x, mine, 1)
    for k in range(1, planes):
        total = total + send(pick(x, lax.rem(mine + k, planes), 1), line_route(k))
    return total


def silu_parts(x):
    s = jax.nn.sigmoid(x)
    return x * s, s * (1.0 + x * (1.0 - s))


def conv_forward(padded, weight, bias, length):
    pre_act = jnp.zeros((length, padded.shape[1]), F32) + bias
    for k in range(CONV):
        pre_act = pre_act + weight[k][None, :] * padded[k : k + length]
    return pre_act


def conv_backward(grad_padded, weight, length):
    grad = jnp.zeros((length, grad_padded.shape[1]), F32)
    for k in range(CONV):
        grad = grad + weight[k][None, :] * grad_padded[CONV - 1 - k : CONV - 1 - k + length]
    return grad.astype(BF16)


def conv_sums(grad, padded):
    length = grad.shape[0]
    return jnp.stack(
        [jnp.sum(grad * padded[k : k + length], axis=0) for k in range(CONV)]
        + [jnp.sum(grad, axis=0)]
    )


def matmul(x, y, dims):
    return lax.dot_general(x, y, ((dims[:1], dims[1:]), ((), ())), preferred_element_type=F32)


def gate_parts(gate_in, upstream, forget_flags):
    grad_out = -forget_flags.astype(F32)[:, None] * upstream.astype(F32)
    value, slope = silu_parts(gate_in.astype(F32))
    return (grad_out * value).astype(BF16), grad_out * slope


def outputs(grad_seq, grad_gate, grad_dtw, sums):
    return (
        grad_seq, grad_gate, grad_dtw,
        sums[:CONV], sums[CONV], sums[CONV + 1], sums[CONV + 3 :], sums[CONV + 2],
    )


def plane_body(
    seq_in, gate_in, upstream, forget_flags, conv_weight, conv_bias,
    proj_weight, dt_weight, dt_bias, a_log, skip_gain,
):
    rim = CONV - 1
    core = lax.axis_index("mp")
    planes = lax.axis_size("ctx") // PLANE
    here = core.astype(jnp.int32).reshape(1)
    rows, dt_rows = seq_in.shape[0], dt_weight.shape[0]
    half = PLANE * rows // 2
    packed = by_owner(seq_in, dt_weight)
    proj_blocks = line_blocks(proj_weight.T)
    moved = in_plane(packed)
    before = rim_before(seq_in[rows - rim :])
    weight, bias, step_bias, rates, gain = (
        own_channels(x)
        for x in (conv_weight, conv_bias[None], dt_bias[None], a_log, skip_gain[None])
    )
    act = conv_head(moved, before, weight, bias, rows)
    dt_plane = moved[:, rows:].reshape(PLANE * dt_rows, -1)
    grad_mixed, _ = gate_parts(gate_in, upstream, forget_flags)
    mixed_packed = by_owner(grad_mixed)
    grad_mixed = in_plane(after(mixed_packed, moved)).reshape(PLANE * rows, -1)

    proj_blocks = after(tuple(proj_blocks), act, mixed_packed, dt_plane)
    rows_proj = place_blocks(proj_blocks, 1)
    dt_blocks = line_blocks(dt_plane)
    part = lambda at: matmul(rows_proj, lax.dynamic_slice_in_dim(act, at * half, half), (1, 1))
    mine, other = sum_plane(part(core), swap_mp(part(1 - core).astype(BF16)))
    rows_dt = place_blocks(dt_blocks, 0)
    step, sig, state, adjoint, bc = scan_local(
        here, mine, other, rows_dt, step_bias, act, grad_mixed, rates
    )
    low = by_halves(mine[:RANK].astype(BF16), other[:RANK].astype(BF16))
    carries = line_carries(state, adjoint, rates)
    mixed, grad_pre, grad_act, grad_rate, grad_vecs, grad_mine, grad_other = scan_full(
        here, bc, rows_dt, step, sig, act, grad_mixed, rates, carries, gain
    )

    dtw_sums = matmul(low, grad_pre, (1, 0)).astype(BF16)
    dtw_moved = along_line(dtw_sums.reshape(planes, RANK // planes, -1))
    mine, other = sum_plane(grad_mine, swap_mp(after(grad_other, dtw_sums)))
    mine, other = mine.astype(BF16), other.astype(BF16)
    packed, grad_conv, early = conv_tail(
        here, mine, other, rows_proj, grad_act, moved, before, weight, bias, dtw_moved
    )
    grad_gate = in_plane(after(mixed, mine).reshape(PLANE, rows, -1))
    returned = in_plane(after(packed, grad_gate))
    grad_gate = gate_gradient(after(grad_gate, packed), gate_in, upstream, forget_flags)
    late = late_rows(after(early, grad_gate))
    sums = jnp.concatenate([grad_conv, grad_vecs, grad_rate], axis=0)
    sums = sum_line(after(sums, grad_gate))
    grad_seq, grad_dtw = to_tokens(returned, (rows, BF16), (dt_rows, F32), late=late)
    return outputs(grad_seq, grad_gate, grad_dtw, sums)


def block_body(
    seq_in, gate_in, upstream, forget_flags, conv_weight, conv_bias,
    proj_weight, dt_weight, dt_bias, a_log, skip_gain,
):
    length = seq_in.shape[0]
    rim = CONV - 1
    padded = jnp.concatenate([shifted(seq_in[length - rim :], "ctx", 1), seq_in], axis=0)
    pre_act = conv_forward(padded, conv_weight, conv_bias[None], length)
    act = jax.nn.silu(pre_act).astype(BF16)
    rows_proj = lax.all_gather(proj_weight, "ctx", axis=0, tiled=True)
    rows_dt = lax.all_gather(dt_weight, "ctx", axis=0, tiled=True)
    projected = lax.psum(matmul(rows_proj, act, (0, 1)), "mp")
    low = projected[:RANK].astype(BF16)
    halves = (jnp.zeros((1,), jnp.int32), projected[:, : length // 2], projected[:, length // 2 :])
    grad_mixed, gate_factor = gate_parts(gate_in, upstream, forget_flags)
    step, sig, state, adjoint, bc = scan_local(
        *halves, rows_dt, dt_bias[None], act, grad_mixed, a_log
    )
    carries = exchange_carries(jnp.concatenate([state[:STATE], adjoint], axis=0), a_log)
    mixed, grad_pre, grad_act, grad_rate, grad_vecs, first, second = scan_full(
        halves[0], bc, rows_dt, step, sig, act, grad_mixed, a_log, carries, skip_gain[None]
    )
    grad_gate = (gate_factor * mixed.astype(F32)).astype(BF16)
    grad_proj = lax.psum(jnp.concatenate([first, second], axis=1), "mp").astype(BF16)
    grad_pre_act = (grad_act + matmul(grad_proj, rows_proj, (0, 1))) * silu_parts(pre_act)[1]
    grad_padded = jnp.concatenate([grad_pre_act, shifted(grad_pre_act[:rim], "ctx", -1)], axis=0)
    grad_seq = conv_backward(grad_padded, conv_weight, length)
    scatter = lambda x, axis: lax.psum_scatter(x, "ctx", scatter_dimension=axis, tiled=True)
    grad_dtw = scatter(matmul(low, grad_pre, (1, 0)), 0)
    sums = scatter(
        jnp.concatenate([conv_sums(grad_pre_act, padded), grad_vecs, grad_rate], axis=0), 1
    )
    return outputs(grad_seq, grad_gate, grad_dtw, sums)


def solution(mesh):
    shares = mesh.shape["mp"] == 2 and mesh.shape["ctx"] in (8, 16)
    body = plane_body if shares else block_body
    return jax.shard_map(
        body,
        mesh=mesh,
        in_specs=(
            P("ctx", "mp"),
            P("ctx", "mp"),
            P("ctx", "mp"),
            P("ctx"),
            P(None, "mp"),
            P("mp"),
            P(("mp", "ctx"), None),
            P("ctx", "mp"),
            P("mp"),
            P(None, "mp"),
            P("mp"),
        ),
        out_specs=(
            P("ctx", "mp"),
            P("ctx", "mp"),
            P("ctx", "mp"),
            P(None, ("mp", "ctx")),
            P(("mp", "ctx")),
            P(("mp", "ctx")),
            P(None, ("mp", "ctx")),
            P(("mp", "ctx")),
        ),
        check_vma=False,
    )
```
